512 devices in a mesh: wide: 64 (over z_lo, x, core), rows: 8 (over z_hi, y).
Axes of the slice: x: 4, y: 4, z: 16 (z_hi: 2, z_lo: 8; z = z_hi * 8 + z_lo), core: 2. Of those that a mesh axis runs over, the one named last changes fastest.
Arguments:
- cotangent: float32 [2, 32768, 3072], P(None, 'wide', 'rows'), may hold values from -6 to 6
- amplitude: bfloat16 [256, 256, 3072], P('wide', None, 'rows'), may hold values from 0.099609375 to 2
- view_phase: bfloat16 [256, 256, 3072], P('wide', None, 'rows'), may hold values from -3.140625 to 3.140625
- layer_block: int32 [256, 256, 384], P('wide', None, 'rows'), may hold values from 0 to 8
- layer_phase: float32 [8, 256], P(None, 'wide'), may hold values from -3.140625 to 3.140625
Outputs:
- grad_amplitude: bfloat16 [256, 256, 3072], P('wide', None, 'rows')
- grad_phase: bfloat16 [256, 256, 3072], P('wide', None, 'rows')
- grad_layers: float32 [8, 256], P(None, 'wide')
The draws below stay inside these ranges and needn't reach their ends.
Inputs may be any that keep to these rules, and one draw needn't show every extreme that they name: `layer_block`: value 8 marks a view occluded in that block of 8 rows.
All inputs are finite; a program needn't handle non-finite values.
Results may differ from the reference program's by a relative error of at most 0.0049.
Values may be sent and summed in bfloat16 or wider, within the bound.
A program may use at most 64 MiB of HBM per device.

```python
import math
import jax
import jax.numpy as jnp
from jax import lax

HOG = 256
LAYERS = 8
BLOCK = 8
NR = 3072
NC = 32768
NH = 256


def with_ends(result, key, smallest, top_value):
    shape = result.shape
    spot = [jax.random.randint(jax.random.fold_in(key, axis), (), 0, shape[axis]) for axis in range(len(shape))]
    result = result.at[tuple(spot)].set(smallest)
    longest = shape.index(max(shape))
    spot[longest] = (spot[longest] + 1) % shape[longest]
    return result.at[tuple(spot)].set(top_value)


def shard_levels(stream_key, shape, split, least, largest):
    level = 1.0
    for position, parts in split:
        heights = jax.random.uniform(jax.random.fold_in(jax.random.fold_in(stream_key, 6), position), (parts,), jnp.float32, least / len(split), largest / len(split))
        level = level * jnp.repeat(jnp.exp(heights), shape[position] // parts).reshape((-1,) + (1,) * (len(shape) - 1 - position))
    return level


def noise(own_key, extent, scale, reach, cuts=(), kind=jnp.bfloat16):
    result = scale * jax.random.normal(own_key, extent, jnp.float32)
    if cuts:
        result = result * shard_levels(own_key, extent, cuts, -0.22, 0.18)
    return jnp.clip(result, -reach, reach).astype(kind)


def setup_inputs(seed: int = 0) -> dict:
    keys = jax.random.split(jax.random.key(seed), 6)
    cotangent = noise(keys[0], (2, NC, NR), 1.0, 6.0, ((1, 64), (2, 8)), jnp.float32)
    amplitude = jnp.clip(jnp.exp(math.log(2.0) - 2.9996462 * jax.random.uniform(keys[1], (HOG, NH, NR), jnp.float32) ** shard_levels(keys[1], (HOG, NH, NR), ((0, 64), (2, 8)), -0.2, 0.2)), 0.099609375, 2.0).astype(jnp.bfloat16)
    view_phase = jnp.clip(jax.random.uniform(keys[2], (HOG, NH, NR), jnp.float32, -3.140625, 3.140625), -3.140625, 3.140625).astype(jnp.bfloat16)
    layer_block = with_ends(jax.random.randint(keys[3], (HOG, NH, NR // BLOCK), 0, LAYERS + 1), jax.random.fold_in(keys[3], 1), 0, LAYERS).astype(jnp.int32)
    layer_phase = jnp.clip(jax.random.uniform(keys[4], (LAYERS, HOG), jnp.float32, -3.140625, 3.140625), -3.140625, 3.140625)
    return {"cotangent": cotangent, "amplitude": amplitude, "view_phase": view_phase, "layer_block": layer_block, "layer_phase": layer_phase}


def fourier_table():
    index = jnp.arange(HOG, dtype=jnp.int32)
    product = index[:, None] * index[None, :] % HOG
    angles = 2.0 * math.pi / HOG * product.astype(jnp.float32)
    samples = index.astype(jnp.float32)
    window = jnp.sin(math.pi * (samples + 0.5) / HOG) ** 2 / math.sqrt(HOG)
    cosine = jnp.cos(angles) * window[None, :]
    sine_part = jnp.sin(angles) * window[None, :]
    return jnp.stack([jnp.stack([cosine, sine_part], 1), jnp.stack([-sine_part, cosine], 1)], 0)

def hogel_frames(extended, count):
    half_hogel = HOG // 2
    rows_here = extended.shape[1]
    left = extended[:, :, :count * half_hogel].reshape(2, rows_here, count, half_hogel)
    right = extended[:, :, half_hogel:(count + 1) * half_hogel].reshape(2, rows_here, count, half_hogel)
    return jnp.concatenate([left, right], 3)

def transform(table, frames):
    return jnp.einsum('pkqn,qrhn->pkhr', table, frames, precision=lax.Precision.HIGHEST)

def view_gradients(real_part, imag_part, amplitude, view_phase, layer_here, phase_table):
    layers_rows = jnp.repeat(layer_here, BLOCK, axis=2)
    visible = (layers_rows < LAYERS).astype(jnp.float32)
    lookup = jnp.zeros(layers_rows.shape, jnp.float32)
    for level in range(LAYERS):
        lookup = lookup + jnp.where(layers_rows == level, phase_table[level][:, None, None], 0.0)
    angles = view_phase.astype(jnp.float32) + lookup
    cosine = jnp.cos(angles)
    sine_part = jnp.sin(angles)
    real_f = real_part.astype(jnp.float32)
    imag_f = imag_part.astype(jnp.float32)
    grad_amp = visible * (real_f * cosine + imag_f * sine_part)
    phase_term = visible * amplitude.astype(jnp.float32) * (imag_f * cosine - real_f * sine_part)
    table_part = jnp.stack([lax.optimization_barrier(jnp.sum(jnp.where(layers_rows == level, phase_term, 0.0), (1, 2))) for level in range(LAYERS)], 0)
    return (grad_amp.astype(jnp.bfloat16), phase_term.astype(jnp.bfloat16), table_part)

def reference(cotangent, amplitude, view_phase, layer_block, layer_phase):
    table = fourier_table()
    half_hogel = HOG // 2
    groups = NR // BLOCK
    row_major = jnp.swapaxes(cotangent, 1, 2)
    padded = jnp.pad(row_major, ((0, 0), (0, 0), (0, half_hogel)))
    strips = jnp.moveaxis(padded.reshape(2, groups, BLOCK, NC + half_hogel), 1, 0)
    amp_groups = jnp.moveaxis(amplitude.reshape(HOG, NH, groups, BLOCK), 2, 0)
    phase_groups = jnp.moveaxis(view_phase.reshape(HOG, NH, groups, BLOCK), 2, 0)
    layer_groups = jnp.moveaxis(layer_block, 2, 0)[..., None]

    def advance(total, pieces):
        strip, amp_here, phase_here, layer_here = pieces
        spectra = transform(table, hogel_frames(strip, NH)).astype(jnp.bfloat16)
        grad_amp, grad_ph, table_part = view_gradients(spectra[0], spectra[1], amp_here, phase_here, layer_here, layer_phase)
        return (total + table_part, (grad_amp, grad_ph))
    start = jnp.zeros((LAYERS, HOG), jnp.float32)
    total, (grad_amp, grad_ph) = lax.scan(advance, start, (strips, amp_groups, phase_groups, layer_groups))
    grad_amp = jnp.moveaxis(grad_amp, 0, 2).reshape(HOG, NH, NR)
    grad_ph = jnp.moveaxis(grad_ph, 0, 2).reshape(HOG, NH, NR)
    return (grad_amp, grad_ph, total / math.sqrt(NR * NH))
```

```python
import functools
import math

import jax
import jax.numpy as jnp
import numpy as np
from jax import lax
from jax.experimental import pallas as pl
from jax.experimental.pallas import tpu as pltpu
from jax.sharding import PartitionSpec as P

MESH = pl.DeviceIdType.MESH
HOG = 256
HALF = HOG // 2
LAYERS = 8
BLOCK = 8
WIDE = 64
ROWS = 8
VIEWS = 4
HOGELS = 4
NR = 384
NB = NR // BLOCK
NH = 256
GROUP = 4
GROUPS = WIDE // GROUP
COS = (0.999999989, -0.499999891, 0.0416664892, -0.00138878035, 2.47698825e-05, -2.70790202e-07, 1.72450525e-09)
SIN = (0.999999999, -0.166666659, 0.00833332129, -0.000198405341, 2.75358492e-06, -2.47288044e-08, 1.36130722e-10)


def fourier_table():
    index = np.arange(HOG)
    angles = 2.0 * math.pi / HOG * (index[:, None] * index[None, :] % HOG)
    window = np.sin(math.pi * (index + 0.5) / HOG) ** 2 / math.sqrt(HOG)
    cosine = np.cos(angles) * window[None, :]
    sine = np.sin(angles) * window[None, :]
    table = np.stack([np.stack([cosine, sine], 1), np.stack([-sine, cosine], 1)], 0)
    table = table.reshape(2, WIDE, VIEWS, 2 * HOG).swapaxes(0, 1).reshape(2 * HOG, 2 * HOG)
    return table.astype(np.float32)


def places(shape):
    return (lax.broadcasted_iota(jnp.int32, shape, axis) for axis in range(2))


def ones_where(chosen):
    return jnp.where(chosen, 1.0, 0.0).astype(jnp.bfloat16)


def gather_order():
    goes, came = places((128, 128))
    part, view, source, half, hogel = goes >> 6, (goes >> 4) & 3, (goes >> 2) & 3, (goes >> 1) & 1, goes & 1
    return ones_where(came == half * 64 + source * 16 + hogel * 8 + part * 4 + view)


def polynomial(coefficients, square):
    total = jnp.full_like(square, coefficients[-1])
    for coefficient in coefficients[-2::-1]:
        total = total * square + coefficient
    return total


def cos_sin(angle):
    square = angle * angle
    return polynomial(COS, square), angle * polynomial(SIN, square)


def halves(value):
    high = value.astype(jnp.bfloat16)
    return high, (value - high.astype(jnp.float32)).astype(jnp.bfloat16)


def dot(a, b):
    return jnp.dot(a, b, preferred_element_type=jnp.float32)


def kernel(
    cot_hbm, amp_hbm, phase_hbm, layer_hbm, table_ref, fourier_hbm,
    grad_amp_hbm, grad_phase_hbm, grad_layers_ref,
    cot, amp, phase, layer_in, fourier, layer, thigh, tlow, spread, gather, order,
    xhigh, xlow, stage, recv, cosines, sines, grad_amp, grad_phase, sums, partial,
    load_sem, send_sem, recv_sem, own_sem, halo_send, halo_recv, out_sem, row_send, row_recv,
):
    me = lax.axis_index("wide")
    row = lax.axis_index("rows")

    barrier = pltpu.get_barrier_semaphore()

    def greet_wide(n, carry):
        other = lax.rem(me + n, WIDE)
        pl.semaphore_signal(barrier, inc=1, device_id={"wide": other}, device_id_type=MESH)
        return carry

    lax.fori_loop(1, WIDE, greet_wide, 0)
    for n in range(1, ROWS):
        pl.semaphore_signal(barrier, inc=1, device_id={"rows": lax.rem(row + n, ROWS)}, device_id_type=MESH)

    loads = [
        pltpu.make_async_copy(source, target, load_sem.at[i])
        for i, (source, target) in enumerate(
            (
                (cot_hbm, cot), (fourier_hbm, fourier), (amp_hbm, amp), (phase_hbm, phase), (layer_hbm, layer_in),
            )
        )
    ]
    for load in loads:
        load.start()
    loads[0].wait()
    high, low = halves(cot[...])
    xhigh[:, : HOGELS * HALF, :] = high
    xlow[...] = low
    loads[1].wait()
    thigh[...], tlow[...] = halves(fourier[...])

    def transform(hogel):
        total = None
        for q in range(2):
            columns = pl.ds(q * HOG, HOG)
            upper = xhigh[q, hogel * HALF : hogel * HALF + HOG, :]
            terms = [dot(thigh[:, columns], upper), dot(tlow[:, columns], upper)]
            if hogel < HOGELS - 1:
                terms.append(dot(thigh[:, columns], xlow[q, hogel * HALF : hogel * HALF + HOG, :]))
            else:
                terms.append(dot(thigh[:, q * HOG : q * HOG + HALF], xlow[q, hogel * HALF :, :]))
            for term in terms:
                total = term if total is None else total + term
        return total.reshape(WIDE, 8, NR)

    def send(half, n):
        other = lax.rem(me + n, WIDE)
        return pltpu.make_async_remote_copy(
            src_ref=stage.at[half, other], dst_ref=recv.at[half, me], send_sem=send_sem.at[half],
            recv_sem=recv_sem.at[half, me], device_id={"wide": other}, device_id_type=MESH,
        )

    def keep(half):
        return pltpu.make_async_copy(stage.at[half, me], recv.at[half, me], own_sem.at[half])

    def each_send(half, act):
        def step(n, carry):
            act(send(half, n))
            return carry

        lax.fori_loop(1, WIDE, step, 0)

    halo = pltpu.make_async_remote_copy(
        src_ref=xhigh.at[:, pl.ds(0, HALF)], dst_ref=xhigh.at[:, pl.ds(HOGELS * HALF, HALF)],
        send_sem=halo_send, recv_sem=halo_recv,
        device_id={"wide": lax.rem(me + WIDE - 1, WIDE)}, device_id_type=MESH,
    )

    stage[0] = jnp.concatenate([transform(0), transform(1)], 1).astype(jnp.bfloat16)
    pl.semaphore_wait(barrier, WIDE - 1 + ROWS - 1)

    @pl.when(me > 0)
    def _():
        halo.start()

    each_send(0, lambda copy: copy.start())
    keep(0).start()
    second = transform(2)

    @pl.when(me < WIDE - 1)
    def _():
        halo.wait_recv()

    @pl.when(me == WIDE - 1)
    def _():
        xhigh[:, pl.ds(HOGELS * HALF, HALF), :] = jnp.zeros((2, HALF, NR), jnp.bfloat16)

    stage[1] = jnp.concatenate([second, transform(3)], 1).astype(jnp.bfloat16)
    each_send(1, lambda copy: copy.start())
    keep(1).start()

    for load in loads[2:]:
        load.wait()
    sums[...] = jnp.zeros_like(sums)
    order[...] = gather_order()
    block, sample = places((NB, NR))
    spread[...] = ones_where(block == sample >> 3)
    sample, block = places((NR, NB))
    gather[...] = ones_where(block == sample >> 3)
    left, right = places((NB, NB))
    same = ones_where(left == right)

    def turned(value, by):
        return lax.dot_general(value, by, (((0,), (0,)), ((), ())), preferred_element_type=jnp.float32)

    for view in range(VIEWS):
        level = layer_in[view]
        layer[view] = turned(level.astype(jnp.float32).astype(jnp.bfloat16), same)
        added = jnp.zeros(level.shape, jnp.float32)
        for l in range(LAYERS):
            added = jnp.where(level == l, table_ref[view, l], added)
        cosine, sine = cos_sin(added)
        seen = level < LAYERS
        cosines[view] = sum(turned(part, spread[...]) for part in halves(jnp.where(seen, cosine, 0.0)))
        sines[view] = sum(turned(part, spread[...]) for part in halves(jnp.where(seen, sine, 0.0)))

    def angles(group, carry):
        here = pl.ds(pl.multiple_of(group * 16, 16), 16)
        own_cosine, own_sine = cos_sin(phase[:, here, :].astype(jnp.float32))
        wide_cosine, wide_sine = cosines[:, here, :], sines[:, here, :]
        cosines[:, here, :] = own_cosine * wide_cosine - own_sine * wide_sine
        sines[:, here, :] = own_sine * wide_cosine + own_cosine * wide_sine
        return carry

    lax.fori_loop(0, GROUPS, angles, 0)

    def finished(group):
        here = pl.ds(pl.multiple_of(group * 16, 16), 16)
        return [
            pltpu.make_async_copy(source.at[:, here], target.at[:, here], out_sem.at[i])
            for i, (source, target) in enumerate(((grad_amp, grad_amp_hbm), (grad_phase, grad_phase_hbm)))
        ]

    keep(0).wait()
    keep(1).wait()

    def gradients(n, carry):
        group = lax.rem(me // GROUP + GROUPS - n, GROUPS)
        here = pl.ds(pl.multiple_of(group * 16, 16), 16)
        for source in range(GROUP):
            index = group * GROUP + source

            @pl.when(index != me)
            def _():
                for half in range(2):
                    landed = recv.at[half, index]
                    pltpu.make_async_copy(landed, landed, recv_sem.at[half, index]).wait()

        came = recv[:, pl.ds(group * GROUP, GROUP), :, :].reshape(2 * GROUP * 16, NR)
        ordered = dot(order[...], came)
        real = ordered[:64].reshape(VIEWS, 16, NR)
        imag = ordered[64:].reshape(VIEWS, 16, NR)
        cosine = cosines[:, here, :]
        sine = sines[:, here, :]
        grad_amp[:, here, :] = (real * cosine + imag * sine).astype(jnp.bfloat16)
        term = amp[:, here, :].astype(jnp.float32) * (imag * cosine - real * sine)
        grad_phase[:, here, :] = term.astype(jnp.bfloat16)
        for copy in finished(group):
            copy.start()
        flat = term.reshape(VIEWS * 16, NR)
        blocks = sum(dot(part, gather[...]) for part in halves(flat)).reshape(VIEWS, 16, NB)
        level = layer[:, here, :]
        for l in range(LAYERS):
            chosen = jnp.where(level == float(l), blocks, 0.0)
            sums[l] += chosen[:, :8, :] + chosen[:, 8:, :]
        return carry

    lax.fori_loop(0, GROUPS, gradients, 0)

    view_of, level_of = places((8, 128))
    own = jnp.zeros((8, 128), jnp.float32)
    for l in range(LAYERS):
        lane = jnp.sum(jnp.sum(sums[l], axis=1), axis=1, keepdims=True)
        lane = jnp.concatenate([lane, jnp.zeros((8 - VIEWS, 1), jnp.float32)], 0)
        own = jnp.where(level_of == l, lane, own)
    partial[0] = own
    for n in range(1, ROWS):
        pltpu.make_async_remote_copy(
            src_ref=partial.at[0], dst_ref=partial.at[n], send_sem=row_send.at[n], recv_sem=row_recv.at[n],
            device_id={"rows": lax.rem(row + n, ROWS)}, device_id_type=MESH,
        ).start()

    for half in range(2):
        each_send(half, lambda copy: copy.wait_send())

    @pl.when(me > 0)
    def _():
        halo.wait_send()

    total = own
    for n in range(1, ROWS):
        pltpu.make_async_copy(partial.at[n], partial.at[n], row_recv.at[n]).wait()
    for n in range(1, ROWS):
        total = total + partial[n]
        pltpu.make_async_copy(partial.at[0], partial.at[0], row_send.at[n]).wait()
    grad_layers_ref[...] = (total * (1.0 / math.sqrt(NR * ROWS * NH)))[:VIEWS, :LAYERS]

    for copy in [
        pltpu.make_async_copy(grad_amp, grad_amp_hbm, out_sem.at[0]),
        pltpu.make_async_copy(grad_phase, grad_phase_hbm, out_sem.at[1]),
    ]:
        copy.wait()


def shards(cotangent, amplitude, view_phase, layer_block, layer_phase):
    anywhere = pl.BlockSpec(memory_space=pl.ANY)
    bf16, f32 = jnp.bfloat16, jnp.float32
    dma = pltpu.SemaphoreType.DMA
    grad_amp, grad_phase, grad_layers = pl.pallas_call(
        kernel,
        out_shape=(
            jax.ShapeDtypeStruct((VIEWS, NH, NR), bf16),
            jax.ShapeDtypeStruct((VIEWS, NH, NR), bf16),
            jax.ShapeDtypeStruct((VIEWS, LAYERS), f32),
        ),
        in_specs=[anywhere] * 4 + [pl.BlockSpec(memory_space=pltpu.SMEM), anywhere],
        out_specs=(anywhere, anywhere, pl.BlockSpec(memory_space=pltpu.VMEM)),
        scratch_shapes=[
            pltpu.VMEM((2, HOGELS * HALF, NR), f32),
            pltpu.VMEM((VIEWS, NH, NR), bf16),
            pltpu.VMEM((VIEWS, NH, NR), bf16),
            pltpu.VMEM((VIEWS, NB, NH), jnp.int32),
            pltpu.VMEM((2 * HOG, 2 * HOG), f32),
            pltpu.VMEM((VIEWS, NH, NB), f32),
            pltpu.VMEM((2 * HOG, 2 * HOG), bf16),
            pltpu.VMEM((2 * HOG, 2 * HOG), bf16),
            pltpu.VMEM((NB, NR), bf16),
            pltpu.VMEM((NR, NB), bf16),
            pltpu.VMEM((128, 128), bf16),
            pltpu.VMEM((2, (HOGELS + 1) * HALF, NR), bf16),
            pltpu.VMEM((2, HOGELS * HALF, NR), bf16),
            pltpu.VMEM((2, WIDE, 16, NR), bf16),
            pltpu.VMEM((2, WIDE, 16, NR), bf16),
            pltpu.VMEM((VIEWS, NH, NR), f32),
            pltpu.VMEM((VIEWS, NH, NR), f32),
            pltpu.VMEM((VIEWS, NH, NR), bf16),
            pltpu.VMEM((VIEWS, NH, NR), bf16),
            pltpu.VMEM((LAYERS, VIEWS, 8, NB), f32),
            pltpu.VMEM((ROWS, 8, 128), f32),
            dma((5,)), dma((2,)), dma((2, WIDE)), dma((2,)), dma, dma, dma((2,)), dma((ROWS,)), dma((ROWS,)),
        ],
        compiler_params=pltpu.CompilerParams(
            collective_id=0, has_side_effects=True, vmem_limit_bytes=48 * 1024 * 1024
        ),
    )(cotangent, amplitude, view_phase, jnp.swapaxes(layer_block, 1, 2), layer_phase.T, fourier_table())
    return grad_amp, grad_phase, grad_layers.T


def solution(mesh):
    in_specs = (
        P(None, "wide", "rows"),
        P("wide", None, "rows"),
        P("wide", None, "rows"),
        P("wide", None, "rows"),
        P(None, "wide"),
    )
    out_specs = (P("wide", None, "rows"), P("wide", None, "rows"), P(None, "wide"))
    return jax.shard_map(shards, mesh=mesh, in_specs=in_specs, out_specs=out_specs, check_vma=False)
```

```python
import functools
import math

import jax
import jax.numpy as jnp
import numpy as np
from jax import lax
from jax.experimental import pallas as pl
from jax.experimental.pallas import tpu as pltpu
from jax.sharding import PartitionSpec as P

MESH = pl.DeviceIdType.MESH
HOG = 256
HALF = HOG // 2
LAYERS = 8
BLOCK = 8
WIDE = 64
ROWS = 8
VIEWS = 4
HOGELS = 4
NR = 384
NB = NR // BLOCK
NH = 256
GROUP = 4
GROUPS = WIDE // GROUP
PLANE = 8
PLANES = WIDE // PLANE
ALONG = 4
VISITS = (
    (4, 5, 6, 7, 1, 2, 3, 0), (4, 5, 6, 0, 7, 2, 3, 1), (0, 1, 3, 4, 2, 5, 6, 7), (0, 1, 2, 3, 4, 5, 6, 7),
    (0, 7, 1, 6, 2, 5, 3, 4), (0, 7, 2, 6, 1, 4, 3, 5), (1, 7, 0, 5, 3, 4, 2, 6), (1, 6, 0, 5, 3, 4, 2, 7),
)
ARRIVALS = tuple(tuple(sorted(range(PLANES), key=lambda s: VISITS[s].index(d) // 2)) for d in range(PLANES))
COS = (0.999999989, -0.499999891, 0.0416664892, -0.00138878035, 2.47698825e-05, -2.70790202e-07, 1.72450525e-09)
SIN = (0.999999999, -0.166666659, 0.00833332129, -0.000198405341, 2.75358492e-06, -2.47288044e-08, 1.36130722e-10)


def fourier_table():
    index = np.arange(HOG)
    angles = 2.0 * math.pi / HOG * (index[:, None] * index[None, :] % HOG)
    window = np.sin(math.pi * (index + 0.5) / HOG) ** 2 / math.sqrt(HOG)
    cosine = np.cos(angles) * window[None, :]
    sine = np.sin(angles) * window[None, :]
    table = np.stack([np.stack([cosine, sine], 1), np.stack([-sine, cosine], 1)], 0)
    table = table.reshape(2, WIDE, VIEWS, 2 * HOG).swapaxes(0, 1).reshape(2 * HOG, 2 * HOG)
    return table.astype(np.float32)


def places(shape):
    return (lax.broadcasted_iota(jnp.int32, shape, axis) for axis in range(2))


def ones_where(chosen):
    return jnp.where(chosen, 1.0, 0.0).astype(jnp.bfloat16)


def gather_order():
    goes, came = places((128, 128))
    part, view, source, half, hogel = goes >> 6, (goes >> 4) & 3, (goes >> 2) & 3, (goes >> 1) & 1, goes & 1
    return ones_where(came == half * 64 + source * 16 + hogel * 8 + part * 4 + view)


def polynomial(coefficients, square):
    total = jnp.full_like(square, coefficients[-1])
    for coefficient in coefficients[-2::-1]:
        total = total * square + coefficient
    return total


def cos_sin(angle):
    square = angle * angle
    return polynomial(COS, square), angle * polynomial(SIN, square)


def halves(value):
    high = value.astype(jnp.bfloat16)
    return high, (value - high.astype(jnp.float32)).astype(jnp.bfloat16)


def dot(a, b):
    return jnp.dot(a, b, preferred_element_type=jnp.float32)


def packed(orders, plane):
    code = jnp.int32(0)
    for index, order in enumerate(orders):
        code = jnp.where(plane == index, sum(entry << (3 * i) for i, entry in enumerate(order)), code)
    return code


def entry_of(code, i):
    return (code >> (3 * i)) & 7


def kernel(
    cot_hbm, amp_hbm, phase_hbm, layer_hbm, table_ref, fourier_hbm,
    grad_amp_hbm, grad_phase_hbm, grad_layers_ref,
    cot, amp, phase, layer_in, fourier, layer, spread, gather, order,
    xhigh, xlow, stage, recv, cosines, sines, grad_amp, grad_phase, sums, partial,
    load_sem, fourier_sem, send_sem, recv_sem, halo_send, halo_recv, out_sem, row_send, row_recv,
    wide_sem, rows_sem,
):
    me = lax.axis_index("wide")
    row = lax.axis_index("rows")
    plane, spot = me // PLANE, lax.rem(me, PLANE)
    upper, along = row // ALONG, lax.rem(row, ALONG)

    def greet(semaphore, **target):
        pl.semaphore_signal(semaphore, inc=1, device_id=target, device_id_type=MESH)

    def beside(n):
        return plane * PLANE + lax.rem(spot + n, PLANE)

    barrier = pltpu.get_barrier_semaphore()
    for n in range(1, PLANES):
        greet(barrier, wide=lax.rem(plane + n, PLANES) * PLANE + spot)
    for n in range(1, PLANE):
        greet(barrier, wide=beside(n))
    for n in range(1, ALONG):
        greet(barrier, rows=upper * ALONG + lax.rem(along + n, ALONG))

    @pl.when(upper == 0)
    def _():
        for n in range(ALONG):
            greet(barrier, rows=ALONG + n)

    visits = packed(VISITS, plane)
    arrivals = packed(ARRIVALS, plane)

    early = pl.ds(0, (HOGELS - 1) * HALF)
    late = pl.ds((HOGELS - 1) * HALF, HALF)
    cot_loads = [
        pltpu.make_async_copy(cot_hbm.at[q, part], cot.at[q, part], load_sem.at[2 * i + q])
        for i, part in enumerate((early, late))
        for q in range(2)
    ]
    loads = [
        pltpu.make_async_copy(source, target, load_sem.at[4 + i])
        for i, (source, target) in enumerate(((amp_hbm, amp), (phase_hbm, phase), (layer_hbm, layer_in)))
    ]

    def rows_of(there):
        return pl.ds(pl.multiple_of(there * 64, 64), 64)

    def fourier_load(i):
        rows = rows_of(entry_of(visits, i))
        return pltpu.make_async_copy(fourier_hbm.at[rows], fourier.at[rows], fourier_sem.at[i])

    for load in cot_loads[:2]:
        load.start()
    for i in range(2):
        fourier_load(i).start()
    for load in cot_loads[2:]:
        load.start()
    for i in range(2, PLANES):
        fourier_load(i).start()
    for load in loads:
        load.start()

    def ready(part, copies):
        for copy in copies:
            copy.wait()
        high, low = halves(cot[:, part, :])
        xhigh[:, part, :] = high
        xlow[:, part, :] = low

    def transform(there, hogel):
        thigh, tlow = halves(fourier[rows_of(there), :])
        first, last = hogel * HALF, hogel * HALF + HOG
        total = None
        for q in range(2):
            columns = slice(q * HOG, q * HOG + HOG)
            terms = [dot(thigh[:, columns], xhigh[q, first:last, :]), dot(tlow[:, columns], xhigh[q, first:last, :])]
            known = min(last, HOGELS * HALF)
            terms.append(dot(thigh[:, q * HOG : q * HOG + known - first], xlow[q, first:known, :]))
            for term in terms:
                total = term if total is None else total + term
        return total.reshape(PLANE, 8, NR)

    def send(half, other):
        return pltpu.make_async_remote_copy(
            src_ref=stage.at[half, other], dst_ref=recv.at[half, me], send_sem=send_sem.at[half],
            recv_sem=recv_sem.at[half, me // GROUP], device_id={"wide": other}, device_id_type=MESH,
        )

    def keep(half):
        return pltpu.make_async_copy(stage.at[half, me], recv.at[half, me], recv_sem.at[half, me // GROUP])

    def prepare(half, quarter):
        for side in range(2):
            there = entry_of(visits, 2 * quarter + side)
            both = [transform(there, 2 * half + hogel) for hogel in range(2)]
            chunk = pl.ds(pl.multiple_of(there * PLANE, PLANE), PLANE)
            stage[half, chunk] = jnp.concatenate(both, 1).astype(jnp.bfloat16)

    def dispatch(half, quarter):
        def step(n, carry):
            there = entry_of(visits, 2 * quarter + lax.rem(n, 2))
            other = there * PLANE + lax.rem(spot + n // 2, PLANE)

            @pl.when(other != me)
            def _():
                send(half, other).start()

            @pl.when(other == me)
            def _():
                keep(half).start()

            return carry

        lax.fori_loop(0, 2 * PLANE, step, 0)

    halo = pltpu.make_async_remote_copy(
        src_ref=xhigh.at[:, pl.ds(0, HALF)], dst_ref=xhigh.at[:, pl.ds(HOGELS * HALF, HALF)],
        send_sem=halo_send, recv_sem=halo_recv,
        device_id={"wide": lax.rem(me + WIDE - 1, WIDE)}, device_id_type=MESH,
    )

    ready(early, cot_loads[:2])
    for i in range(2):
        fourier_load(i).wait()
    prepare(0, 0)

    pl.semaphore_wait(barrier, PLANES + PLANE + ALONG - 3 + ALONG * upper)
    for n in range(1, PLANE):
        greet(wide_sem, wide=beside(n))

    @pl.when(upper == 1)
    def _():
        for n in range(ALONG):
            greet(rows_sem, rows=n)

    pl.semaphore_wait(wide_sem, PLANE - 1)

    @pl.when(me > 0)
    def _():
        halo.start()

    dispatch(0, 0)
    ready(late, cot_loads[2:])

    @pl.when(me < WIDE - 1)
    def _():
        halo.wait_recv()

    @pl.when(me == WIDE - 1)
    def _():
        xhigh[:, pl.ds(HOGELS * HALF, HALF), :] = jnp.zeros((2, HALF, NR), jnp.bfloat16)

    prepare(1, 0)
    dispatch(1, 0)

    def quarters(quarter, carry):
        for half in range(2):
            prepare(half, quarter)
            dispatch(half, quarter)
        return carry

    for i in range(2, PLANES):
        fourier_load(i).wait()
    lax.fori_loop(1, PLANES // 2, quarters, 0)

    for load in loads:
        load.wait()
    sums[...] = jnp.zeros_like(sums)
    order[...] = gather_order()
    block, sample = places((NB, NR))
    spread[...] = ones_where(block == sample >> 3)
    sample, block = places((NR, NB))
    gather[...] = ones_where(block == sample >> 3)
    left, right = places((NB, NB))
    same = ones_where(left == right)

    def turned(value, by):
        return lax.dot_general(value, by, (((0,), (0,)), ((), ())), preferred_element_type=jnp.float32)

    for view in range(VIEWS):
        level = layer_in[view]
        layer[view] = turned(level.astype(jnp.float32).astype(jnp.bfloat16), same)
        added = jnp.zeros(level.shape, jnp.float32)
        for l in range(LAYERS):
            added = jnp.where(level == l, table_ref[view, l], added)
        cosine, sine = cos_sin(added)
        seen = level < LAYERS
        cosines[view] = sum(turned(part, spread[...]) for part in halves(jnp.where(seen, cosine, 0.0)))
        sines[view] = sum(turned(part, spread[...]) for part in halves(jnp.where(seen, sine, 0.0)))

    def angles(group, carry):
        here = pl.ds(pl.multiple_of(group * 16, 16), 16)
        own_cosine, own_sine = cos_sin(phase[:, here, :].astype(jnp.float32))
        wide_cosine, wide_sine = cosines[:, here, :], sines[:, here, :]
        cosines[:, here, :] = own_cosine * wide_cosine - own_sine * wide_sine
        sines[:, here, :] = own_sine * wide_cosine + own_cosine * wide_sine
        return carry

    lax.fori_loop(0, GROUPS, angles, 0)

    def finished(group):
        here = pl.ds(pl.multiple_of(group * 16, 16), 16)
        return [
            pltpu.make_async_copy(source.at[:, here], target.at[:, here], out_sem.at[i])
            for i, (source, target) in enumerate(((grad_amp, grad_amp_hbm), (grad_phase, grad_phase_hbm)))
        ]

    def gradients(n, carry):
        group = 2 * entry_of(arrivals, n // 2) + lax.rem(n, 2)
        here = pl.ds(pl.multiple_of(group * 16, 16), 16)
        for half in range(2):
            landed = recv.at[half, pl.ds(group * GROUP, GROUP)]
            pltpu.make_async_copy(landed, landed, recv_sem.at[half, group]).wait()
        came = recv[:, pl.ds(group * GROUP, GROUP), :, :].reshape(2 * GROUP * 16, NR)
        ordered = dot(order[...], came)
        real = ordered[:64].reshape(VIEWS, 16, NR)
        imag = ordered[64:].reshape(VIEWS, 16, NR)
        cosine = cosines[:, here, :]
        sine = sines[:, here, :]
        grad_amp[:, here, :] = (real * cosine + imag * sine).astype(jnp.bfloat16)
        term = amp[:, here, :].astype(jnp.float32) * (imag * cosine - real * sine)
        grad_phase[:, here, :] = term.astype(jnp.bfloat16)
        for copy in finished(group):
            copy.start()
        flat = term.reshape(VIEWS * 16, NR)
        blocks = sum(dot(part, gather[...]) for part in halves(flat)).reshape(VIEWS, 16, NB)
        level = layer[:, here, :]
        for l in range(LAYERS):
            chosen = jnp.where(level == float(l), blocks, 0.0)
            sums[l] += chosen[:, :8, :] + chosen[:, 8:, :]
        return carry

    lax.fori_loop(0, GROUPS, gradients, 0)

    view_of, level_of = places((8, 128))
    own = jnp.zeros((8, 128), jnp.float32)
    for l in range(LAYERS):
        lane = jnp.sum(jnp.sum(sums[l], axis=1), axis=1, keepdims=True)
        lane = jnp.concatenate([lane, jnp.zeros((8 - VIEWS, 1), jnp.float32)], 0)
        own = jnp.where(level_of == l, lane, own)
    partial[0] = own

    @pl.when(upper == 0)
    def _():
        pl.semaphore_wait(rows_sem, ALONG)

    for n in range(1, ROWS):
        pltpu.make_async_remote_copy(
            src_ref=partial.at[0], dst_ref=partial.at[n], send_sem=row_send.at[n], recv_sem=row_recv.at[n],
            device_id={"rows": lax.rem(row + n, ROWS)}, device_id_type=MESH,
        ).start()

    for half in range(2):
        gone = stage.at[half, pl.ds(0, WIDE - 1)]
        pltpu.make_async_copy(gone, gone, send_sem.at[half]).wait()

    @pl.when(me > 0)
    def _():
        halo.wait_send()

    total = own
    for n in range(1, ROWS):
        pltpu.make_async_copy(partial.at[n], partial.at[n], row_recv.at[n]).wait()
    for n in range(1, ROWS):
        total = total + partial[n]
        pltpu.make_async_copy(partial.at[0], partial.at[0], row_send.at[n]).wait()
    grad_layers_ref[...] = (total * (1.0 / math.sqrt(NR * ROWS * NH)))[:VIEWS, :LAYERS]

    for copy in [
        pltpu.make_async_copy(grad_amp, grad_amp_hbm, out_sem.at[0]),
        pltpu.make_async_copy(grad_phase, grad_phase_hbm, out_sem.at[1]),
    ]:
        copy.wait()


def hand_over(amp_in, phase_in, layers_in, amp_out, phase_out, layers_out, amp, phase, layers, in_sem, out_sem):
    pieces = [(layers_in, layers, layers_out)]
    for view in range(VIEWS):
        pieces.append((amp_in.at[view], amp.at[view], amp_out.at[view]))
        pieces.append((phase_in.at[view], phase.at[view], phase_out.at[view]))
    arrivals = [pltpu.make_async_copy(p[0], p[1], in_sem.at[i]) for i, p in enumerate(pieces)]
    departures = [pltpu.make_async_copy(p[1], p[2], out_sem.at[i]) for i, p in enumerate(pieces)]
    for copy in arrivals:
        copy.start()
    for arrival, departure in zip(arrivals, departures):
        arrival.wait()
        departure.start()
    for copy in departures:
        copy.wait()


def shards(cotangent, amplitude, view_phase, layer_block, layer_phase):
    anywhere = pl.BlockSpec(memory_space=pl.ANY)
    bf16, f32 = jnp.bfloat16, jnp.float32
    dma = pltpu.SemaphoreType.DMA
    grad_amp, grad_phase, grad_layers = grads = pl.pallas_call(
        kernel,
        out_shape=(
            jax.ShapeDtypeStruct((VIEWS, NH, NR), bf16),
            jax.ShapeDtypeStruct((VIEWS, NH, NR), bf16),
            jax.ShapeDtypeStruct((VIEWS, LAYERS), f32),
        ),
        in_specs=[anywhere] * 4 + [pl.BlockSpec(memory_space=pltpu.SMEM), anywhere],
        out_specs=(anywhere, anywhere, pl.BlockSpec(memory_space=pltpu.VMEM)),
        scratch_shapes=[
            pltpu.VMEM((2, HOGELS * HALF, NR), f32),
            pltpu.VMEM((VIEWS, NH, NR), bf16),
            pltpu.VMEM((VIEWS, NH, NR), bf16),
            pltpu.VMEM((VIEWS, NB, NH), jnp.int32),
            pltpu.VMEM((2 * HOG, 2 * HOG), f32),
            pltpu.VMEM((VIEWS, NH, NB), f32),
            pltpu.VMEM((NB, NR), bf16),
            pltpu.VMEM((NR, NB), bf16),
            pltpu.VMEM((128, 128), bf16),
            pltpu.VMEM((2, (HOGELS + 1) * HALF, NR), bf16),
            pltpu.VMEM((2, HOGELS * HALF, NR), bf16),
            pltpu.VMEM((2, WIDE, 16, NR), bf16),
            pltpu.VMEM((2, WIDE, 16, NR), bf16),
            pltpu.VMEM((VIEWS, NH, NR), f32),
            pltpu.VMEM((VIEWS, NH, NR), f32),
            pltpu.VMEM((VIEWS, NH, NR), bf16),
            pltpu.VMEM((VIEWS, NH, NR), bf16),
            pltpu.VMEM((LAYERS, VIEWS, 8, NB), f32),
            pltpu.VMEM((ROWS, 8, 128), f32),
            dma((7,)), dma((PLANES,)), dma((2,)), dma((2, GROUPS)), dma, dma, dma((2,)), dma((ROWS,)), dma((ROWS,)),
            pltpu.SemaphoreType.REGULAR, pltpu.SemaphoreType.REGULAR,
        ],
        compiler_params=pltpu.CompilerParams(
            collective_id=0, has_side_effects=True, vmem_limit_bytes=62 * 1024 * 1024
        ),
    )(cotangent, amplitude, view_phase, jnp.swapaxes(layer_block, 1, 2), layer_phase.T, fourier_table())
    grad_amp, grad_phase, grad_layers = pl.pallas_call(
        hand_over,
        out_shape=tuple(jax.ShapeDtypeStruct(g.shape, g.dtype) for g in grads),
        in_specs=[anywhere] * 3,
        out_specs=(anywhere,) * 3,
        scratch_shapes=[pltpu.VMEM(g.shape, g.dtype) for g in grads] + [dma((2 * VIEWS + 1,))] * 2,
        compiler_params=pltpu.CompilerParams(vmem_limit_bytes=62 * 1024 * 1024),
    )(*grads)
    return grad_amp, grad_phase, grad_layers.T


def solution(mesh):
    in_specs = (
        P(None, "wide", "rows"),
        P("wide", None, "rows"),
        P("wide", None, "rows"),
        P("wide", None, "rows"),
        P(None, "wide"),
    )
    out_specs = (P("wide", None, "rows"), P("wide", None, "rows"), P(None, "wide"))
    return jax.shard_map(shards, mesh=mesh, in_specs=in_specs, out_specs=out_specs, check_vma=False)
```

```python
import functools
import math

import jax
import jax.numpy as jnp
import numpy as np
from jax import lax
from jax.experimental import pallas as pl
from jax.experimental.pallas import tpu as pltpu
from jax.sharding import PartitionSpec as P

MESH = pl.DeviceIdType.MESH
HOG = 256
HALF = HOG // 2
LAYERS = 8
BLOCK = 8
WIDE = 64
ROWS = 8
VIEWS = 4
HOGELS = 4
NR = 384
NB = NR // BLOCK
NH = 256
GROUP = 4
GROUPS = WIDE // GROUP
PLANE = 8
PLANES = WIDE // PLANE
ALONG = 4
VISITS = (
    (4, 5, 6, 7, 1, 2, 3, 0), (4, 5, 6, 0, 7, 2, 3, 1), (0, 1, 3, 4, 2, 5, 6, 7), (0, 1, 2, 3, 4, 5, 6, 7),
    (0, 7, 1, 6, 2, 5, 3, 4), (0, 7, 2, 6, 1, 4, 3, 5), (1, 7, 0, 5, 3, 4, 2, 6), (0, 6, 1, 5, 3, 4, 2, 7),
    (4, 5, 6, 7, 1, 2, 3, 0), (4, 5, 6, 0, 7, 2, 3, 1), (0, 1, 3, 4, 2, 5, 6, 7), (0, 1, 2, 3, 4, 5, 6, 7),
    (0, 7, 1, 6, 2, 5, 3, 4), (0, 7, 2, 6, 1, 4, 3, 5), (1, 7, 0, 5, 3, 4, 2, 6), (3, 0, 1, 6, 5, 4, 2, 7),
)
LAST, UP, DOWN = PLANES - 1, 4, 3
ARRIVALS = tuple(
    tuple(sorted(range(PLANES), key=lambda s: VISITS[half + s].index(d) // 2)) for half in (0, PLANES) for d in range(PLANES)
)
COS = (0.999999989, -0.499999891, 0.0416664892, -0.00138878035, 2.47698825e-05, -2.70790202e-07, 1.72450525e-09)
SIN = (0.999999999, -0.166666659, 0.00833332129, -0.000198405341, 2.75358492e-06, -2.47288044e-08, 1.36130722e-10)


def fourier_table():
    index = np.arange(HOG)
    angles = 2.0 * math.pi / HOG * (index[:, None] * index[None, :] % HOG)
    window = np.sin(math.pi * (index + 0.5) / HOG) ** 2 / math.sqrt(HOG)
    cosine = np.cos(angles) * window[None, :]
    sine = np.sin(angles) * window[None, :]
    table = np.stack([np.stack([cosine, sine], 1), np.stack([-sine, cosine], 1)], 0)
    table = table.reshape(2, WIDE, VIEWS, 2 * HOG).swapaxes(0, 1).reshape(2 * HOG, 2 * HOG)
    return table.astype(np.float32)


def places(shape):
    return (lax.broadcasted_iota(jnp.int32, shape, axis) for axis in range(2))


def ones_where(chosen):
    return jnp.where(chosen, 1.0, 0.0).astype(jnp.bfloat16)


def gather_order():
    goes, came = places((128, 128))
    part, view, source, half, hogel = goes >> 6, (goes >> 4) & 3, (goes >> 2) & 3, (goes >> 1) & 1, goes & 1
    return ones_where(came == half * 64 + source * 16 + hogel * 8 + part * 4 + view)


def polynomial(coefficients, square):
    total = jnp.full_like(square, coefficients[-1])
    for coefficient in coefficients[-2::-1]:
        total = total * square + coefficient
    return total


def cos_sin(angle):
    square = angle * angle
    return polynomial(COS, square), angle * polynomial(SIN, square)


def halves(value):
    high = value.astype(jnp.bfloat16)
    return high, (value - high.astype(jnp.float32)).astype(jnp.bfloat16)


def dot(a, b):
    return jnp.dot(a, b, preferred_element_type=jnp.float32)


def packed(orders, which):
    code = jnp.int32(0)
    for index, order in enumerate(orders):
        code = jnp.where(which == index, sum(entry << (3 * i) for i, entry in enumerate(order)), code)
    return code


def entry_of(code, i):
    return (code >> (3 * i)) & 7


def kernel(
    cot_hbm, amp_hbm, phase_hbm, layer_hbm, table_hbm, fourier_hbm,
    grad_amp_hbm, grad_phase_hbm, grad_layers_ref,
    cot, amp, phase, layer_in, table_ref, fourier, layer, spread, gather, order,
    xhigh, xlow, stage, recv, lent, cosines, sines, grad_amp, grad_phase, sums, partial,
    load_sem, fourier_sem, send_sem, recv_sem, halo_send, halo_recv, out_sem, row_send, row_recv,
    lent_sem, passed_sem, wide_sem, rows_sem,
):
    me = lax.axis_index("wide")
    row = lax.axis_index("rows")
    plane, spot = me // PLANE, lax.rem(me, PLANE)
    upper, along = row // ALONG, lax.rem(row, ALONG)

    def greet(semaphore, **target):
        pl.semaphore_signal(semaphore, inc=1, device_id=target, device_id_type=MESH)

    def beside(n):
        return plane * PLANE + lax.rem(spot + n, PLANE)

    barrier = pltpu.get_barrier_semaphore()
    for n in range(1, PLANES):
        greet(barrier, wide=lax.rem(plane + n, PLANES) * PLANE + spot)
    for n in range(1, PLANE):
        greet(barrier, wide=beside(n))
    for n in range(1, ALONG):
        greet(barrier, rows=upper * ALONG + lax.rem(along + n, ALONG))

    @pl.when(upper == 0)
    def _():
        for n in range(ALONG):
            greet(barrier, rows=ALONG + n)

    relays = (upper == 0) & (plane == UP)
    relayed = (upper == 1) & (plane == LAST)
    rising = (plane == LAST) | (plane == UP)
    lender, borrower = jnp.where(rising, LAST, 0), jnp.where(rising, DOWN, UP)
    through = jnp.where(rising, UP, DOWN)

    @pl.when(relays)
    def _():
        greet(barrier, wide=lender * PLANE + spot, rows=ALONG + along)

    visits = packed(VISITS, upper * PLANES + plane)
    arrivals = packed(ARRIVALS, upper * PLANES + plane)

    early = pl.ds(0, (HOGELS - 1) * HALF)
    late = pl.ds((HOGELS - 1) * HALF, HALF)
    cot_loads = [
        pltpu.make_async_copy(cot_hbm.at[q, part], cot.at[q, part], load_sem.at[2 * i + q])
        for i, part in enumerate((early, late))
        for q in range(2)
    ]
    loads = [
        pltpu.make_async_copy(source, target, load_sem.at[4 + i])
        for i, (source, target) in enumerate((
            ((amp_hbm, amp), (phase_hbm, phase), (layer_hbm, layer_in), (table_hbm, table_ref))
        ))
    ]

    def rows_of(there):
        return pl.ds(pl.multiple_of(there * 64, 64), 64)

    def fourier_load(i):
        rows = rows_of(entry_of(visits, i))
        return pltpu.make_async_copy(fourier_hbm.at[rows], fourier.at[rows], fourier_sem.at[i])

    for load in cot_loads[:2]:
        load.start()
    for i in range(2):
        fourier_load(i).start()
    for load in cot_loads[2:]:
        load.start()
    for i in range(2, PLANES):
        fourier_load(i).start()
    for load in loads:
        load.start()

    def ready(part, copies):
        for copy in copies:
            copy.wait()
        high, low = halves(cot[:, part, :])
        xhigh[:, part, :] = high
        xlow[:, part, :] = low

    def transform(there, hogel):
        thigh, tlow = halves(fourier[rows_of(there), :])
        first, last = hogel * HALF, hogel * HALF + HOG
        total = None
        for q in range(2):
            columns = slice(q * HOG, q * HOG + HOG)
            terms = [dot(thigh[:, columns], xhigh[q, first:last, :]), dot(tlow[:, columns], xhigh[q, first:last, :])]
            known = min(last, HOGELS * HALF)
            terms.append(dot(thigh[:, q * HOG : q * HOG + known - first], xlow[q, first:known, :]))
            for term in terms:
                total = term if total is None else total + term
        return total.reshape(PLANE, 8, NR)

    def send(half, other):
        return pltpu.make_async_remote_copy(
            src_ref=stage.at[half, other], dst_ref=recv.at[half, me], send_sem=send_sem.at[half],
            recv_sem=recv_sem.at[half, plane], device_id={"wide": other}, device_id_type=MESH,
        )

    def keep(half):
        return pltpu.make_async_copy(stage.at[half, me], recv.at[half, me], recv_sem.at[half, plane])

    def prepare(half, quarter):
        for side in range(2):
            there = entry_of(visits, 2 * quarter + side)
            both = [transform(there, 2 * half + hogel) for hogel in range(2)]
            chunk = pl.ds(pl.multiple_of(there * PLANE, PLANE), PLANE)
            stage[half, chunk] = jnp.concatenate(both, 1).astype(jnp.bfloat16)

    def lend(half):
        return pltpu.make_async_remote_copy(
            src_ref=stage.at[half, pl.ds(borrower * PLANE, PLANE)], dst_ref=lent.at[half], send_sem=send_sem.at[half],
            recv_sem=lent_sem.at[half], device_id={"wide": through * PLANE + spot, "rows": along}, device_id_type=MESH,
        )

    def pass_on(half, n):
        return pltpu.make_async_remote_copy(
            src_ref=lent.at[half, n], dst_ref=recv.at[half, lender * PLANE + spot], send_sem=passed_sem.at[half],
            recv_sem=recv_sem.at[half, lender], device_id={"wide": borrower * PLANE + n, "rows": ALONG + along}, device_id_type=MESH,
        )

    def dispatch(half, quarter):
        @pl.when(relayed & (quarter == 0) & (half == 1))
        def _():
            lend(half).start()

        def step(n, carry):
            there = entry_of(visits, 2 * quarter + lax.rem(n, 2))
            other = there * PLANE + lax.rem(spot + n // 2, PLANE)

            @pl.when((other != me) & ~(relayed & (there == borrower) & (half == 1)))
            def _():
                send(half, other).start()

            @pl.when(other == me)
            def _():
                keep(half).start()

            return carry

        lax.fori_loop(0, 2 * PLANE, step, 0)

    halo = pltpu.make_async_remote_copy(
        src_ref=xhigh.at[:, pl.ds(0, HALF)], dst_ref=xhigh.at[:, pl.ds(HOGELS * HALF, HALF)],
        send_sem=halo_send, recv_sem=halo_recv,
        device_id={"wide": lax.rem(me + WIDE - 1, WIDE)}, device_id_type=MESH,
    )

    ready(early, cot_loads[:2])
    for i in range(2):
        fourier_load(i).wait()
    prepare(0, 0)

    pl.semaphore_wait(barrier, PLANES + PLANE + ALONG - 3 + ALONG * upper + relayed.astype(jnp.int32))
    for n in range(1, PLANE):
        greet(wide_sem, wide=beside(n))

    @pl.when(upper == 1)
    def _():
        for n in range(ALONG):
            greet(rows_sem, rows=n)

    pl.semaphore_wait(wide_sem, PLANE - 1)

    @pl.when(me > 0)
    def _():
        halo.start()

    dispatch(0, 0)
    ready(late, cot_loads[2:])

    @pl.when(me < WIDE - 1)
    def _():
        halo.wait_recv()

    @pl.when(me == WIDE - 1)
    def _():
        xhigh[:, pl.ds(HOGELS * HALF, HALF), :] = jnp.zeros((2, HALF, NR), jnp.bfloat16)

    prepare(1, 0)
    dispatch(1, 0)

    def quarters(quarter, carry):
        for half in range(2):
            prepare(half, quarter)
            dispatch(half, quarter)
        return carry

    for i in range(2, PLANES):
        fourier_load(i).wait()
    lax.fori_loop(1, PLANES // 2, quarters, 0)

    for load in loads:
        load.wait()
    sums[...] = jnp.zeros_like(sums)
    order[...] = gather_order()
    block, sample = places((NB, NR))
    spread[...] = ones_where(block == sample >> 3)
    sample, block = places((NR, NB))
    gather[...] = ones_where(block == sample >> 3)
    left, right = places((NB, NB))
    same = ones_where(left == right)

    def turned(value, by):
        return lax.dot_general(value, by, (((0,), (0,)), ((), ())), preferred_element_type=jnp.float32)

    for view in range(VIEWS):
        level = layer_in[view]
        layer[view] = turned(level.astype(jnp.float32).astype(jnp.bfloat16), same)
        added = jnp.zeros(level.shape, jnp.float32)
        for l in range(LAYERS):
            added = jnp.where(level == l, table_ref[view, l], added)
        cosine, sine = cos_sin(added)
        seen = level < LAYERS
        cosines[view] = sum(turned(part, spread[...]) for part in halves(jnp.where(seen, cosine, 0.0)))
        sines[view] = sum(turned(part, spread[...]) for part in halves(jnp.where(seen, sine, 0.0)))

    def angles(group, carry):
        here = pl.ds(pl.multiple_of(group * 16, 16), 16)
        own_cosine, own_sine = cos_sin(phase[:, here, :].astype(jnp.float32))
        wide_cosine, wide_sine = cosines[:, here, :], sines[:, here, :]
        cosines[:, here, :] = own_cosine * wide_cosine - own_sine * wide_sine
        sines[:, here, :] = own_sine * wide_cosine + own_cosine * wide_sine
        return carry

    lax.fori_loop(0, GROUPS, angles, 0)

    @pl.when(relays)
    def _():
        for half in (1,):
            pltpu.make_async_copy(lent.at[half], lent.at[half], lent_sem.at[half]).wait()

            def forward(n, carry):
                pass_on(half, n).start()
                return carry

            lax.fori_loop(0, PLANE, forward, 0)

    def finished(here):
        return [
            pltpu.make_async_copy(source.at[:, here], target.at[:, here], out_sem.at[i])
            for i, (source, target) in enumerate(((grad_amp, grad_amp_hbm), (grad_phase, grad_phase_hbm)))
        ]

    def gradients(n, carry):
        origin = entry_of(arrivals, n)
        hogels = PLANE * HOGELS
        here = pl.ds(pl.multiple_of(origin * hogels, hogels), hogels)
        for half in range(2):
            landed = recv.at[half, pl.ds(origin * PLANE, PLANE)]
            pltpu.make_async_copy(landed, landed, recv_sem.at[half, origin]).wait()
        came = [
            recv[:, pl.ds(origin * PLANE + first, GROUP), :, :].reshape(2 * GROUP * 16, NR) for first in (0, GROUP)
        ]
        ordered = dot(order[...], jnp.concatenate(came, 1))

        def part(rows):
            return jnp.concatenate([ordered[rows, i * NR : (i + 1) * NR].reshape(VIEWS, 16, NR) for i in range(2)], 1)

        real, imag = part(slice(0, 64)), part(slice(64, 128))
        cosine = cosines[:, here, :]
        sine = sines[:, here, :]
        term = amp[:, here, :].astype(jnp.float32) * (imag * cosine - real * sine)
        flat = term.reshape(VIEWS * hogels, NR)
        blocks = sum(dot(part, gather[...]) for part in halves(flat)).reshape(VIEWS, hogels, NB)
        grad_amp[:, here, :] = (real * cosine + imag * sine).astype(jnp.bfloat16)
        grad_phase[:, here, :] = term.astype(jnp.bfloat16)
        for copy in finished(here):
            copy.start()
        level = layer[:, here, :]
        for l in range(LAYERS):
            chosen = jnp.where(level == float(l), blocks, 0.0)
            sums[l] += jnp.sum(chosen.reshape(VIEWS, hogels // 8, 8, NB), axis=1)
        return carry

    lax.fori_loop(0, PLANES, gradients, 0)

    view_of, level_of = places((8, 128))
    own = jnp.zeros((8, 128), jnp.float32)
    for l in range(LAYERS):
        lane = jnp.sum(jnp.sum(sums[l], axis=1), axis=1, keepdims=True)
        lane = jnp.concatenate([lane, jnp.zeros((8 - VIEWS, 1), jnp.float32)], 0)
        own = jnp.where(level_of == l, lane, own)
    partial[0] = own

    @pl.when(upper == 0)
    def _():
        pl.semaphore_wait(rows_sem, ALONG)

    for n in range(1, ROWS):
        pltpu.make_async_remote_copy(
            src_ref=partial.at[0], dst_ref=partial.at[n], send_sem=row_send.at[n], recv_sem=row_recv.at[n],
            device_id={"rows": lax.rem(row + n, ROWS)}, device_id_type=MESH,
        ).start()

    for half in range(2):
        gone = stage.at[half, pl.ds(0, WIDE - 1)]
        pltpu.make_async_copy(gone, gone, send_sem.at[half]).wait()

    @pl.when(relays)
    def _():
        for half in (1,):
            pltpu.make_async_copy(lent.at[half], lent.at[half], passed_sem.at[half]).wait()

    @pl.when(me > 0)
    def _():
        halo.wait_send()

    total = own
    for n in range(1, ROWS):
        pltpu.make_async_copy(partial.at[n], partial.at[n], row_recv.at[n]).wait()
    for n in range(1, ROWS):
        total = total + partial[n]
        pltpu.make_async_copy(partial.at[0], partial.at[0], row_send.at[n]).wait()
    grad_layers_ref[...] = (total * (1.0 / math.sqrt(NR * ROWS * NH)))[:VIEWS, :LAYERS]

    for copy in [
        pltpu.make_async_copy(grad_amp, grad_amp_hbm, out_sem.at[0]),
        pltpu.make_async_copy(grad_phase, grad_phase_hbm, out_sem.at[1]),
    ]:
        copy.wait()


def hand_over(amp_in, phase_in, layers_in, amp_out, phase_out, layers_out, amp, phase, layers, in_sem, out_sem):
    pieces = [(layers_in, layers, layers_out)]
    for view in range(VIEWS):
        pieces.append((amp_in.at[view], amp.at[view], amp_out.at[view]))
        pieces.append((phase_in.at[view], phase.at[view], phase_out.at[view]))
    arrivals = [pltpu.make_async_copy(p[0], p[1], in_sem.at[i]) for i, p in enumerate(pieces)]
    departures = [pltpu.make_async_copy(p[1], p[2], out_sem.at[i]) for i, p in enumerate(pieces)]
    for copy in arrivals:
        copy.start()
    for arrival, departure in zip(arrivals, departures):
        arrival.wait()
        departure.start()
    for copy in departures:
        copy.wait()


def shards(cotangent, amplitude, view_phase, layer_block, layer_phase):
    anywhere = pl.BlockSpec(memory_space=pl.ANY)
    bf16, f32 = jnp.bfloat16, jnp.float32
    dma = pltpu.SemaphoreType.DMA
    grad_amp, grad_phase, grad_layers = grads = pl.pallas_call(
        kernel,
        out_shape=(
            jax.ShapeDtypeStruct((VIEWS, NH, NR), bf16),
            jax.ShapeDtypeStruct((VIEWS, NH, NR), bf16),
            jax.ShapeDtypeStruct((VIEWS, LAYERS), f32),
        ),
        in_specs=[anywhere] * 6,
        out_specs=(anywhere, anywhere, pl.BlockSpec(memory_space=pltpu.VMEM)),
        scratch_shapes=[
            pltpu.VMEM((2, HOGELS * HALF, NR), f32),
            pltpu.VMEM((VIEWS, NH, NR), bf16),
            pltpu.VMEM((VIEWS, NH, NR), bf16),
            pltpu.VMEM((VIEWS, NB, NH), jnp.int32),
            pltpu.SMEM((VIEWS, LAYERS), f32),
            pltpu.VMEM((2 * HOG, 2 * HOG), f32),
            pltpu.VMEM((VIEWS, NH, NB), f32),
            pltpu.VMEM((NB, NR), bf16),
            pltpu.VMEM((NR, NB), bf16),
            pltpu.VMEM((128, 128), bf16),
            pltpu.VMEM((2, (HOGELS + 1) * HALF, NR), bf16),
            pltpu.VMEM((2, HOGELS * HALF, NR), bf16),
            pltpu.VMEM((2, WIDE, 16, NR), bf16),
            pltpu.VMEM((2, WIDE, 16, NR), bf16),
            pltpu.VMEM((2, PLANE, 16, NR), bf16),
            pltpu.VMEM((VIEWS, NH, NR), f32),
            pltpu.VMEM((VIEWS, NH, NR), f32),
            pltpu.VMEM((VIEWS, NH, NR), bf16),
            pltpu.VMEM((VIEWS, NH, NR), bf16),
            pltpu.VMEM((LAYERS, VIEWS, 8, NB), f32),
            pltpu.VMEM((ROWS, 8, 128), f32),
            dma((8,)), dma((PLANES,)), dma((2,)), dma((2, PLANES)), dma, dma, dma((2,)), dma((ROWS,)), dma((ROWS,)),
            dma((2,)), dma((2,)), pltpu.SemaphoreType.REGULAR, pltpu.SemaphoreType.REGULAR,
        ],
        compiler_params=pltpu.CompilerParams(
            collective_id=0, has_side_effects=True, vmem_limit_bytes=62 * 1024 * 1024
        ),
    )(cotangent, amplitude, view_phase, jnp.swapaxes(layer_block, 1, 2), layer_phase.T, fourier_table())
    grad_amp, grad_phase, grad_layers = pl.pallas_call(
        hand_over,
        out_shape=tuple(jax.ShapeDtypeStruct(g.shape, g.dtype) for g in grads),
        in_specs=[anywhere] * 3,
        out_specs=(anywhere,) * 3,
        scratch_shapes=[pltpu.VMEM(g.shape, g.dtype) for g in grads] + [dma((2 * VIEWS + 1,))] * 2,
        compiler_params=pltpu.CompilerParams(vmem_limit_bytes=62 * 1024 * 1024),
    )(*grads)
    return grad_amp, grad_phase, grad_layers.T


def solution(mesh):
    in_specs = (
        P(None, "wide", "rows"),
        P("wide", None, "rows"),
        P("wide", None, "rows"),
        P("wide", None, "rows"),
        P(None, "wide"),
    )
    out_specs = (P("wide", None, "rows"), P("wide", None, "rows"), P(None, "wide"))
    return jax.shard_map(shards, mesh=mesh, in_specs=in_specs, out_specs=out_specs, check_vma=False)
```

```python
import functools
import math

import jax
import jax.numpy as jnp
import numpy as np
from jax import lax
from jax.experimental import pallas as pl
from jax.experimental.pallas import tpu as pltpu
from jax.sharding import PartitionSpec as P

MESH = pl.DeviceIdType.MESH
HOG = 256
HALF = HOG // 2
LAYERS = 8
BLOCK = 8
WIDE = 64
ROWS = 8
VIEWS = 4
HOGELS = 4
NR = 384
NB = NR // BLOCK
NH = 256
GROUP = 4
GROUPS = WIDE // GROUP
PLANE = 8
PLANES = WIDE // PLANE
ALONG = 4
VISITS = (
    (4, 5, 6, 7, 1, 2, 3, 0), (4, 5, 6, 0, 7, 2, 3, 1), (0, 1, 3, 4, 2, 5, 6, 7), (0, 1, 2, 3, 4, 5, 6, 7),
    (0, 7, 1, 6, 2, 5, 3, 4), (0, 7, 2, 6, 1, 4, 3, 5), (1, 7, 0, 5, 3, 4, 2, 6), (0, 6, 1, 5, 3, 4, 2, 7),
    (4, 5, 6, 7, 1, 2, 3, 0), (4, 5, 6, 0, 7, 2, 3, 1), (0, 1, 3, 4, 2, 5, 6, 7), (0, 1, 2, 3, 4, 5, 6, 7),
    (0, 7, 1, 6, 2, 5, 3, 4), (0, 7, 2, 6, 1, 4, 3, 5), (1, 7, 0, 5, 3, 4, 2, 6), (3, 0, 1, 6, 5, 4, 2, 7),
)
LAST, UP, DOWN = PLANES - 1, 4, 3
ARRIVALS = tuple(
    tuple(sorted(range(PLANES), key=lambda s: VISITS[half + s].index(d) // 2)) for half in (0, PLANES) for d in range(PLANES)
)
COS = (0.999999989, -0.499999891, 0.0416664892, -0.00138878035, 2.47698825e-05, -2.70790202e-07, 1.72450525e-09)
SIN = (0.999999999, -0.166666659, 0.00833332129, -0.000198405341, 2.75358492e-06, -2.47288044e-08, 1.36130722e-10)


def fourier_table():
    index = np.arange(HOG)
    angles = 2.0 * math.pi / HOG * (index[:, None] * index[None, :] % HOG)
    window = np.sin(math.pi * (index + 0.5) / HOG) ** 2 / math.sqrt(HOG)
    cosine = np.cos(angles) * window[None, :]
    sine = np.sin(angles) * window[None, :]
    table = np.stack([np.stack([cosine, sine], 1), np.stack([-sine, cosine], 1)], 0)
    table = table.reshape(2, WIDE, VIEWS, 2 * HOG).swapaxes(0, 1).reshape(2 * HOG, 2 * HOG)
    return table.astype(np.float32)


def places(shape):
    return (lax.broadcasted_iota(jnp.int32, shape, axis) for axis in range(2))


def ones_where(chosen):
    return jnp.where(chosen, 1.0, 0.0).astype(jnp.bfloat16)


def gather_order():
    goes, came = places((128, 128))
    part, view, source, half, hogel = goes >> 6, (goes >> 4) & 3, (goes >> 2) & 3, (goes >> 1) & 1, goes & 1
    return ones_where(came == half * 64 + source * 16 + hogel * 8 + part * 4 + view)


def polynomial(coefficients, square):
    total = jnp.full_like(square, coefficients[-1])
    for coefficient in coefficients[-2::-1]:
        total = total * square + coefficient
    return total


def cos_sin(angle):
    square = angle * angle
    return polynomial(COS, square), angle * polynomial(SIN, square)


def halves(value):
    high = value.astype(jnp.bfloat16)
    return high, (value - high.astype(jnp.float32)).astype(jnp.bfloat16)


def dot(a, b):
    return jnp.dot(a, b, preferred_element_type=jnp.float32)


def packed(orders, which):
    code = jnp.int32(0)
    for index, order in enumerate(orders):
        code = jnp.where(which == index, sum(entry << (3 * i) for i, entry in enumerate(order)), code)
    return code


def entry_of(code, i):
    return (code >> (3 * i)) & 7


def kernel(
    cot_hbm, amp_hbm, phase_hbm, layer_hbm, table_hbm, fourier_hbm,
    grad_amp, grad_phase, grad_layers_ref,
    cot, amp, phase, layer_in, table_ref, fourier, layer, spread, gather, order,
    xhigh, xlow, stage, recv, lent, cosines, sines, sums, partial,
    load_sem, fourier_sem, send_sem, recv_sem, halo_send, halo_recv, row_send, row_recv,
    lent_sem, passed_sem, wide_sem, rows_sem,
):
    me = lax.axis_index("wide")
    row = lax.axis_index("rows")
    plane, spot = me // PLANE, lax.rem(me, PLANE)
    upper, along = row // ALONG, lax.rem(row, ALONG)

    def greet(semaphore, **target):
        pl.semaphore_signal(semaphore, inc=1, device_id=target, device_id_type=MESH)

    def beside(n):
        return plane * PLANE + lax.rem(spot + n, PLANE)

    barrier = pltpu.get_barrier_semaphore()
    for n in range(1, PLANES):
        greet(barrier, wide=lax.rem(plane + n, PLANES) * PLANE + spot)
    for n in range(1, PLANE):
        greet(barrier, wide=beside(n))
    for n in range(1, ALONG):
        greet(barrier, rows=upper * ALONG + lax.rem(along + n, ALONG))

    @pl.when(upper == 0)
    def _():
        for n in range(ALONG):
            greet(barrier, rows=ALONG + n)

    relays = (upper == 0) & (plane == UP)
    relayed = (upper == 1) & (plane == LAST)
    rising = (plane == LAST) | (plane == UP)
    lender, borrower = jnp.where(rising, LAST, 0), jnp.where(rising, DOWN, UP)
    through = jnp.where(rising, UP, DOWN)

    @pl.when(relays)
    def _():
        greet(barrier, wide=lender * PLANE + spot, rows=ALONG + along)

    visits = packed(VISITS, upper * PLANES + plane)
    arrivals = packed(ARRIVALS, upper * PLANES + plane)

    early = pl.ds(0, (HOGELS - 1) * HALF)
    late = pl.ds((HOGELS - 1) * HALF, HALF)
    cot_loads = [
        pltpu.make_async_copy(cot_hbm.at[q, part], cot.at[q, part], load_sem.at[2 * i + q])
        for i, part in enumerate((early, late))
        for q in range(2)
    ]
    loads = [
        pltpu.make_async_copy(source, target, load_sem.at[4 + i])
        for i, (source, target) in enumerate((
            ((amp_hbm, amp), (phase_hbm, phase), (layer_hbm, layer_in), (table_hbm, table_ref))
        ))
    ]

    def rows_of(there):
        return pl.ds(pl.multiple_of(there * 64, 64), 64)

    def fourier_load(i):
        rows = rows_of(entry_of(visits, i))
        return pltpu.make_async_copy(fourier_hbm.at[rows], fourier.at[rows], fourier_sem.at[i])

    for load in cot_loads[:2]:
        load.start()
    for i in range(2):
        fourier_load(i).start()
    for load in cot_loads[2:]:
        load.start()
    for i in range(2, PLANES):
        fourier_load(i).start()
    for load in loads:
        load.start()

    def ready(part, copies):
        for copy in copies:
            copy.wait()
        high, low = halves(cot[:, part, :])
        xhigh[:, part, :] = high
        xlow[:, part, :] = low

    def transform(there, hogel):
        thigh, tlow = halves(fourier[rows_of(there), :])
        first, last = hogel * HALF, hogel * HALF + HOG
        total = None
        for q in range(2):
            columns = slice(q * HOG, q * HOG + HOG)
            terms = [dot(thigh[:, columns], xhigh[q, first:last, :]), dot(tlow[:, columns], xhigh[q, first:last, :])]
            known = min(last, HOGELS * HALF)
            terms.append(dot(thigh[:, q * HOG : q * HOG + known - first], xlow[q, first:known, :]))
            for term in terms:
                total = term if total is None else total + term
        return total.reshape(PLANE, 8, NR)

    def send(half, other):
        return pltpu.make_async_remote_copy(
            src_ref=stage.at[half, other], dst_ref=recv.at[half, me], send_sem=send_sem.at[half],
            recv_sem=recv_sem.at[half, plane], device_id={"wide": other}, device_id_type=MESH,
        )

    def keep(half):
        return pltpu.make_async_copy(stage.at[half, me], recv.at[half, me], recv_sem.at[half, plane])

    def prepare(half, quarter):
        for side in range(2):
            there = entry_of(visits, 2 * quarter + side)
            both = [transform(there, 2 * half + hogel) for hogel in range(2)]
            chunk = pl.ds(pl.multiple_of(there * PLANE, PLANE), PLANE)
            stage[half, chunk] = jnp.concatenate(both, 1).astype(jnp.bfloat16)

    def lend(half):
        return pltpu.make_async_remote_copy(
            src_ref=stage.at[half, pl.ds(borrower * PLANE, PLANE)], dst_ref=lent.at[half], send_sem=send_sem.at[half],
            recv_sem=lent_sem.at[half], device_id={"wide": through * PLANE + spot, "rows": along}, device_id_type=MESH,
        )

    def pass_on(half, n):
        return pltpu.make_async_remote_copy(
            src_ref=lent.at[half, n], dst_ref=recv.at[half, lender * PLANE + spot], send_sem=passed_sem.at[half],
            recv_sem=recv_sem.at[half, lender], device_id={"wide": borrower * PLANE + n, "rows": ALONG + along}, device_id_type=MESH,
        )

    def dispatch(half, quarter):
        @pl.when(relayed & (quarter == 0) & (half == 1))
        def _():
            lend(half).start()

        def step(n, carry):
            there = entry_of(visits, 2 * quarter + lax.rem(n, 2))
            other = there * PLANE + lax.rem(spot + n // 2, PLANE)

            @pl.when((other != me) & ~(relayed & (there == borrower) & (half == 1)))
            def _():
                send(half, other).start()

            @pl.when(other == me)
            def _():
                keep(half).start()

            return carry

        lax.fori_loop(0, 2 * PLANE, step, 0)

    halo = pltpu.make_async_remote_copy(
        src_ref=xhigh.at[:, pl.ds(0, HALF)], dst_ref=xhigh.at[:, pl.ds(HOGELS * HALF, HALF)],
        send_sem=halo_send, recv_sem=halo_recv,
        device_id={"wide": lax.rem(me + WIDE - 1, WIDE)}, device_id_type=MESH,
    )

    ready(early, cot_loads[:2])
    for i in range(2):
        fourier_load(i).wait()
    prepare(0, 0)

    pl.semaphore_wait(barrier, PLANES + PLANE + ALONG - 3 + ALONG * upper + relayed.astype(jnp.int32))
    for n in range(1, PLANE):
        greet(wide_sem, wide=beside(n))

    @pl.when(upper == 1)
    def _():
        for n in range(ALONG):
            greet(rows_sem, rows=n)

    pl.semaphore_wait(wide_sem, PLANE - 1)

    @pl.when(me > 0)
    def _():
        halo.start()

    dispatch(0, 0)
    ready(late, cot_loads[2:])

    @pl.when(me < WIDE - 1)
    def _():
        halo.wait_recv()

    @pl.when(me == WIDE - 1)
    def _():
        xhigh[:, pl.ds(HOGELS * HALF, HALF), :] = jnp.zeros((2, HALF, NR), jnp.bfloat16)

    prepare(1, 0)
    dispatch(1, 0)

    def quarters(quarter, carry):
        for half in range(2):
            prepare(half, quarter)
            dispatch(half, quarter)
        return carry

    for i in range(2, PLANES):
        fourier_load(i).wait()
    lax.fori_loop(1, PLANES // 2, quarters, 0)

    for load in loads:
        load.wait()
    sums[...] = jnp.zeros_like(sums)
    order[...] = gather_order()
    block, sample = places((NB, NR))
    spread[...] = ones_where(block == sample >> 3)
    sample, block = places((NR, NB))
    gather[...] = ones_where(block == sample >> 3)
    left, right = places((NB, NB))
    same = ones_where(left == right)

    def turned(value, by):
        return lax.dot_general(value, by, (((0,), (0,)), ((), ())), preferred_element_type=jnp.float32)

    for view in range(VIEWS):
        level = layer_in[view]
        layer[view] = turned(level.astype(jnp.float32).astype(jnp.bfloat16), same)
        added = jnp.zeros(level.shape, jnp.float32)
        for l in range(LAYERS):
            added = jnp.where(level == l, table_ref[view, l], added)
        cosine, sine = cos_sin(added)
        seen = level < LAYERS
        cosines[view] = sum(turned(part, spread[...]) for part in halves(jnp.where(seen, cosine, 0.0)))
        sines[view] = sum(turned(part, spread[...]) for part in halves(jnp.where(seen, sine, 0.0)))

    def angles(group, carry):
        here = pl.ds(pl.multiple_of(group * 16, 16), 16)
        own_cosine, own_sine = cos_sin(phase[:, here, :].astype(jnp.float32))
        wide_cosine, wide_sine = cosines[:, here, :], sines[:, here, :]
        cosines[:, here, :] = own_cosine * wide_cosine - own_sine * wide_sine
        sines[:, here, :] = own_sine * wide_cosine + own_cosine * wide_sine
        return carry

    lax.fori_loop(0, GROUPS, angles, 0)

    @pl.when(relays)
    def _():
        for half in (1,):
            pltpu.make_async_copy(lent.at[half], lent.at[half], lent_sem.at[half]).wait()

            def forward(n, carry):
                pass_on(half, n).start()
                return carry

            lax.fori_loop(0, PLANE, forward, 0)

    def gradients(n, carry):
        origin = entry_of(arrivals, n)
        hogels = PLANE * HOGELS
        here = pl.ds(pl.multiple_of(origin * hogels, hogels), hogels)
        for half in range(2):
            landed = recv.at[half, pl.ds(origin * PLANE, PLANE)]
            pltpu.make_async_copy(landed, landed, recv_sem.at[half, origin]).wait()
        came = [
            recv[:, pl.ds(origin * PLANE + first, GROUP), :, :].reshape(2 * GROUP * 16, NR) for first in (0, GROUP)
        ]
        ordered = dot(order[...], jnp.concatenate(came, 1))

        def part(rows):
            return jnp.concatenate([ordered[rows, i * NR : (i + 1) * NR].reshape(VIEWS, 16, NR) for i in range(2)], 1)

        real, imag = part(slice(0, 64)), part(slice(64, 128))
        cosine = cosines[:, here, :]
        sine = sines[:, here, :]
        term = amp[:, here, :].astype(jnp.float32) * (imag * cosine - real * sine)
        flat = term.reshape(VIEWS * hogels, NR)
        blocks = sum(dot(part, gather[...]) for part in halves(flat)).reshape(VIEWS, hogels, NB)
        grad_amp[:, here, :] = (real * cosine + imag * sine).astype(jnp.bfloat16)
        grad_phase[:, here, :] = term.astype(jnp.bfloat16)
        level = layer[:, here, :]
        for l in range(LAYERS):
            chosen = jnp.where(level == float(l), blocks, 0.0)
            sums[l] += jnp.sum(chosen.reshape(VIEWS, hogels // 8, 8, NB), axis=1)
        return carry

    lax.fori_loop(0, PLANES, gradients, 0)

    view_of, level_of = places((8, 128))
    own = jnp.zeros((8, 128), jnp.float32)
    for l in range(LAYERS):
        lane = jnp.sum(jnp.sum(sums[l], axis=1), axis=1, keepdims=True)
        lane = jnp.concatenate([lane, jnp.zeros((8 - VIEWS, 1), jnp.float32)], 0)
        own = jnp.where(level_of == l, lane, own)
    partial[0] = own

    @pl.when(upper == 0)
    def _():
        pl.semaphore_wait(rows_sem, ALONG)

    for n in range(1, ROWS):
        pltpu.make_async_remote_copy(
            src_ref=partial.at[0], dst_ref=partial.at[n], send_sem=row_send.at[n], recv_sem=row_recv.at[n],
            device_id={"rows": lax.rem(row + n, ROWS)}, device_id_type=MESH,
        ).start()

    for half in range(2):
        gone = stage.at[half, pl.ds(0, WIDE - 1)]
        pltpu.make_async_copy(gone, gone, send_sem.at[half]).wait()

    @pl.when(relays)
    def _():
        for half in (1,):
            pltpu.make_async_copy(lent.at[half], lent.at[half], passed_sem.at[half]).wait()

    @pl.when(me > 0)
    def _():
        halo.wait_send()

    total = own
    for n in range(1, ROWS):
        pltpu.make_async_copy(partial.at[n], partial.at[n], row_recv.at[n]).wait()
    for n in range(1, ROWS):
        total = total + partial[n]
        pltpu.make_async_copy(partial.at[0], partial.at[0], row_send.at[n]).wait()
    grad_layers_ref[...] = (total * (1.0 / math.sqrt(NR * ROWS * NH)))[:VIEWS, :LAYERS]


def hand_over(amp_in, phase_in, layers_in, amp_out, phase_out, layers_out, sem):
    copies = [pltpu.make_async_copy(layers_in, layers_out, sem.at[2 * VIEWS])]
    for view in range(VIEWS):
        copies.append(pltpu.make_async_copy(amp_in.at[view], amp_out.at[view], sem.at[view]))
        copies.append(pltpu.make_async_copy(phase_in.at[view], phase_out.at[view], sem.at[VIEWS + view]))
    for copy in copies:
        copy.start()
    for copy in copies:
        copy.wait()


def shards(cotangent, amplitude, view_phase, layer_block, layer_phase):
    anywhere = pl.BlockSpec(memory_space=pl.ANY)
    bf16, f32 = jnp.bfloat16, jnp.float32
    dma = pltpu.SemaphoreType.DMA
    grad_amp, grad_phase, grad_layers = grads = pl.pallas_call(
        kernel,
        out_shape=(
            pltpu.VMEM((VIEWS, NH, NR), bf16),
            pltpu.VMEM((VIEWS, NH, NR), bf16),
            pltpu.VMEM((VIEWS, LAYERS), f32),
        ),
        in_specs=[anywhere] * 6,
        out_specs=(pl.BlockSpec(memory_space=pltpu.VMEM),) * 3,
        scratch_shapes=[
            pltpu.VMEM((2, HOGELS * HALF, NR), f32),
            pltpu.VMEM((VIEWS, NH, NR), bf16),
            pltpu.VMEM((VIEWS, NH, NR), bf16),
            pltpu.VMEM((VIEWS, NB, NH), jnp.int32),
            pltpu.SMEM((VIEWS, LAYERS), f32),
            pltpu.VMEM((2 * HOG, 2 * HOG), f32),
            pltpu.VMEM((VIEWS, NH, NB), f32),
            pltpu.VMEM((NB, NR), bf16),
            pltpu.VMEM((NR, NB), bf16),
            pltpu.VMEM((128, 128), bf16),
            pltpu.VMEM((2, (HOGELS + 1) * HALF, NR), bf16),
            pltpu.VMEM((2, HOGELS * HALF, NR), bf16),
            pltpu.VMEM((2, WIDE, 16, NR), bf16),
            pltpu.VMEM((2, WIDE, 16, NR), bf16),
            pltpu.VMEM((2, PLANE, 16, NR), bf16),
            pltpu.VMEM((VIEWS, NH, NR), f32),
            pltpu.VMEM((VIEWS, NH, NR), f32),
            pltpu.VMEM((LAYERS, VIEWS, 8, NB), f32),
            pltpu.VMEM((ROWS, 8, 128), f32),
            dma((8,)), dma((PLANES,)), dma((2,)), dma((2, PLANES)), dma, dma, dma((ROWS,)), dma((ROWS,)),
            dma((2,)), dma((2,)), pltpu.SemaphoreType.REGULAR, pltpu.SemaphoreType.REGULAR,
        ],
        compiler_params=pltpu.CompilerParams(
            collective_id=0, has_side_effects=True, vmem_limit_bytes=61 * 1024 * 1024
        ),
    )(cotangent, amplitude, view_phase, jnp.swapaxes(layer_block, 1, 2), layer_phase.T, fourier_table())
    grad_amp, grad_phase, grad_layers = pl.pallas_call(
        hand_over,
        out_shape=tuple(jax.ShapeDtypeStruct(g.shape, g.dtype) for g in grads),
        in_specs=[pl.BlockSpec(memory_space=pltpu.VMEM)] * 3,
        out_specs=(anywhere,) * 3,
        scratch_shapes=[dma((2 * VIEWS + 1,))],
    )(*(pltpu.with_memory_space_constraint(g, pltpu.VMEM) for g in grads))
    return grad_amp, grad_phase, grad_layers.T


def solution(mesh):
    in_specs = (
        P(None, "wide", "rows"),
        P("wide", None, "rows"),
        P("wide", None, "rows"),
        P("wide", None, "rows"),
        P(None, "wide"),
    )
    out_specs = (P("wide", None, "rows"), P("wide", None, "rows"), P(None, "wide"))
    return jax.shard_map(shards, mesh=mesh, in_specs=in_specs, out_specs=out_specs, check_vma=False)
```

```python
import functools
import math

import jax
import jax.numpy as jnp
import numpy as np
from jax import lax
from jax.experimental import pallas as pl
from jax.experimental.pallas import tpu as pltpu
from jax.sharding import PartitionSpec as P

MESH = pl.DeviceIdType.MESH
HOG = 256
HALF = HOG // 2
LAYERS = 8
BLOCK = 8
WIDE = 64
ROWS = 8
VIEWS = 4
HOGELS = 4
NR = 384
NB = NR // BLOCK
NH = 256
GROUP = 4
GROUPS = WIDE // GROUP
PLANE = 8
PLANES = WIDE // PLANE
ALONG = 4
VISITS = (
    (4, 5, 6, 7, 1, 2, 3, 0),
    (4, 6, 7, 0, 5, 2, 3, 1),
    (0, 1, 3, 4, 2, 7, 6, 5),
    (0, 1, 2, 3, 4, 5, 6, 7),
    (0, 7, 1, 6, 2, 5, 3, 4),
    (0, 7, 2, 6, 1, 4, 3, 5),
    (1, 7, 0, 5, 3, 4, 2, 6),
    (0, 6, 1, 5, 3, 4, 2, 7),
    (4, 5, 6, 7, 1, 2, 3, 0),
    (4, 6, 7, 0, 5, 2, 3, 1),
    (0, 1, 3, 4, 2, 7, 6, 5),
    (0, 1, 2, 3, 4, 5, 6, 7),
    (0, 7, 1, 6, 2, 5, 3, 4),
    (0, 7, 2, 6, 1, 4, 3, 5),
    (1, 7, 0, 5, 3, 4, 2, 6),
    (3, 0, 1, 6, 5, 4, 2, 7),
)
LAST, UP, DOWN = PLANES - 1, 4, 3
LENT = (1,)
ARRIVALS = tuple(
    tuple(sorted(range(PLANES), key=lambda s: VISITS[half + s].index(d) // 2)) for half in (0, PLANES) for d in range(PLANES)
)
COS = (0.999999989, -0.499999891, 0.0416664892, -0.00138878035, 2.47698825e-05, -2.70790202e-07, 1.72450525e-09)
SIN = (0.999999999, -0.166666659, 0.00833332129, -0.000198405341, 2.75358492e-06, -2.47288044e-08, 1.36130722e-10)


def fourier_table():
    index = np.arange(HOG)
    angles = 2.0 * math.pi / HOG * (index[:, None] * index[None, :] % HOG)
    window = np.sin(math.pi * (index + 0.5) / HOG) ** 2 / math.sqrt(HOG)
    cosine = np.cos(angles) * window[None, :]
    sine = np.sin(angles) * window[None, :]
    table = np.stack([np.stack([cosine, sine], 1), np.stack([-sine, cosine], 1)], 0)
    table = table.reshape(2, WIDE, VIEWS, 2 * HOG).swapaxes(0, 1).reshape(2 * HOG, 2 * HOG)
    return table.astype(np.float32)


def places(shape):
    return (lax.broadcasted_iota(jnp.int32, shape, axis) for axis in range(2))


def ones_where(chosen):
    return jnp.where(chosen, 1.0, 0.0).astype(jnp.bfloat16)


def gather_order():
    goes, came = places((128, 128))
    part, view, source, half, hogel = goes >> 6, (goes >> 4) & 3, (goes >> 2) & 3, (goes >> 1) & 1, goes & 1
    return ones_where(came == half * 64 + source * 16 + hogel * 8 + part * 4 + view)


def polynomial(coefficients, square):
    total = jnp.full_like(square, coefficients[-1])
    for coefficient in coefficients[-2::-1]:
        total = total * square + coefficient
    return total


def cos_sin(angle):
    square = angle * angle
    return polynomial(COS, square), angle * polynomial(SIN, square)


def halves(value):
    high = value.astype(jnp.bfloat16)
    return high, (value - high.astype(jnp.float32)).astype(jnp.bfloat16)


def dot(a, b):
    return jnp.dot(a, b, preferred_element_type=jnp.float32)


def packed(orders, which):
    code = jnp.int32(0)
    for index, order in enumerate(orders):
        code = jnp.where(which == index, sum(entry << (3 * i) for i, entry in enumerate(order)), code)
    return code


def entry_of(code, i):
    return (code >> (3 * i)) & 7


def kernel(
    cot_hbm, amp_hbm, phase_hbm, layer_hbm, table_hbm, fourier_hbm,
    grad_amp, grad_phase, grad_layers_ref,
    cot, amp, phase, layer_in, table_ref, fourier, layer, spread, gather, order,
    xhigh, xlow, stage, recv, lent, cosines, sines, sums, partial,
    load_sem, fourier_sem, send_sem, recv_sem, halo_send, halo_recv, row_send, row_recv,
    lent_sem, passed_sem, wide_sem, rows_sem,
):
    me = lax.axis_index("wide")
    row = lax.axis_index("rows")
    plane, spot = me // PLANE, lax.rem(me, PLANE)
    upper, along = row // ALONG, lax.rem(row, ALONG)

    def greet(semaphore, **target):
        pl.semaphore_signal(semaphore, inc=1, device_id=target, device_id_type=MESH)

    def beside(n):
        return plane * PLANE + lax.rem(spot + n, PLANE)

    barrier = pltpu.get_barrier_semaphore()
    for n in range(1, PLANES):
        greet(barrier, wide=lax.rem(plane + n, PLANES) * PLANE + spot)
    for n in range(1, PLANE):
        greet(barrier, wide=beside(n))
    for n in range(1, ALONG):
        greet(barrier, rows=upper * ALONG + lax.rem(along + n, ALONG))

    @pl.when(upper == 0)
    def _():
        for n in range(ALONG):
            greet(barrier, rows=ALONG + n)

    relays = (upper == 0) & (plane == UP)
    relayed = (upper == 1) & (plane == LAST)
    rising = (plane == LAST) | (plane == UP)
    lender, borrower = jnp.where(rising, LAST, 0), jnp.where(rising, DOWN, UP)
    through = jnp.where(rising, UP, DOWN)

    @pl.when(relays)
    def _():
        greet(barrier, wide=lender * PLANE + spot, rows=ALONG + along)

    visits = packed(VISITS, upper * PLANES + plane)
    arrivals = packed(ARRIVALS, upper * PLANES + plane)

    early = pl.ds(0, (HOGELS - 1) * HALF)
    late = pl.ds((HOGELS - 1) * HALF, HALF)
    cot_loads = [
        pltpu.make_async_copy(cot_hbm.at[q, part], cot.at[q, part], load_sem.at[2 * i + q])
        for i, part in enumerate((early, late))
        for q in range(2)
    ]
    loads = [
        pltpu.make_async_copy(source, target, load_sem.at[4 + i])
        for i, (source, target) in enumerate((
            ((amp_hbm, amp), (phase_hbm, phase), (layer_hbm, layer_in), (table_hbm, table_ref))
        ))
    ]

    def rows_of(there):
        return pl.ds(pl.multiple_of(there * 64, 64), 64)

    def fourier_load(i):
        rows = rows_of(entry_of(visits, i))
        return pltpu.make_async_copy(fourier_hbm.at[rows], fourier.at[rows], fourier_sem.at[i])

    for load in cot_loads[:2]:
        load.start()
    for i in range(2):
        fourier_load(i).start()
    for load in cot_loads[2:]:
        load.start()
    for i in range(2, PLANES):
        fourier_load(i).start()
    for load in loads:
        load.start()

    def ready(part, copies):
        for copy in copies:
            copy.wait()
        high, low = halves(cot[:, part, :])
        xhigh[:, part, :] = high
        xlow[:, part, :] = low

    def transform(there, hogel):
        thigh, tlow = halves(fourier[rows_of(there), :])
        first, last = hogel * HALF, hogel * HALF + HOG
        total = None
        for q in range(2):
            columns = slice(q * HOG, q * HOG + HOG)
            terms = [dot(thigh[:, columns], xhigh[q, first:last, :]), dot(tlow[:, columns], xhigh[q, first:last, :])]
            known = min(last, HOGELS * HALF)
            terms.append(dot(thigh[:, q * HOG : q * HOG + known - first], xlow[q, first:known, :]))
            for term in terms:
                total = term if total is None else total + term
        return total.reshape(PLANE, 8, NR)

    def send(half, other):
        return pltpu.make_async_remote_copy(
            src_ref=stage.at[half, other], dst_ref=recv.at[half, me], send_sem=send_sem.at[half],
            recv_sem=recv_sem.at[half, plane], device_id={"wide": other}, device_id_type=MESH,
        )

    def keep(half):
        return pltpu.make_async_copy(stage.at[half, me], recv.at[half, me], recv_sem.at[half, plane])

    def prepare(half, quarter):
        for side in range(2):
            there = entry_of(visits, 2 * quarter + side)
            both = [transform(there, 2 * half + hogel) for hogel in range(2)]
            chunk = pl.ds(pl.multiple_of(there * PLANE, PLANE), PLANE)
            stage[half, chunk] = jnp.concatenate(both, 1).astype(jnp.bfloat16)

    def lend(half):
        return pltpu.make_async_remote_copy(
            src_ref=stage.at[half, pl.ds(borrower * PLANE, PLANE)], dst_ref=lent.at[half], send_sem=send_sem.at[half],
            recv_sem=lent_sem.at[half], device_id={"wide": through * PLANE + spot, "rows": along}, device_id_type=MESH,
        )

    def pass_on(half, n):
        return pltpu.make_async_remote_copy(
            src_ref=lent.at[half, n], dst_ref=recv.at[half, lender * PLANE + spot], send_sem=passed_sem.at[half],
            recv_sem=recv_sem.at[half, lender], device_id={"wide": borrower * PLANE + n, "rows": ALONG + along}, device_id_type=MESH,
        )

    def dispatch(half, quarter, first=0, last=2 * PLANE):
        @pl.when(relayed & (quarter == 0) & (half in LENT) & (last > 2))
        def _():
            lend(half).start()

        def step(n, carry):
            there = entry_of(visits, 2 * quarter + lax.rem(n, 2))
            other = there * PLANE + lax.rem(spot + n // 2, PLANE)

            @pl.when((other != me) & ~(relayed & (there == borrower) & (half in LENT)))
            def _():
                send(half, other).start()

            @pl.when(other == me)
            def _():
                keep(half).start()

            return carry

        lax.fori_loop(first, last, step, 0)

    halo = pltpu.make_async_remote_copy(
        src_ref=xhigh.at[:, pl.ds(0, HALF)], dst_ref=xhigh.at[:, pl.ds(HOGELS * HALF, HALF)],
        send_sem=halo_send, recv_sem=halo_recv,
        device_id={"wide": lax.rem(me + WIDE - 1, WIDE)}, device_id_type=MESH,
    )

    ready(early, cot_loads[:2])
    for i in range(2):
        fourier_load(i).wait()
    prepare(0, 0)

    pl.semaphore_wait(barrier, PLANES + PLANE + ALONG - 3 + ALONG * upper + relayed.astype(jnp.int32))
    for n in range(1, PLANE):
        greet(wide_sem, wide=beside(n))

    dispatch(0, 0, 0, 2)
    for i in (2, 3):
        fourier_load(i).wait()
    prepare(0, 1)
    dispatch(0, 1, 0, 2)
    @pl.when(upper == 1)
    def _():
        for n in range(ALONG):
            greet(rows_sem, rows=n)

    pl.semaphore_wait(wide_sem, PLANE - 1)

    @pl.when(me > 0)
    def _():
        halo.start()

    dispatch(0, 0, 2)
    ready(late, cot_loads[2:])

    @pl.when(me < WIDE - 1)
    def _():
        halo.wait_recv()

    @pl.when(me == WIDE - 1)
    def _():
        xhigh[:, pl.ds(HOGELS * HALF, HALF), :] = jnp.zeros((2, HALF, NR), jnp.bfloat16)

    prepare(1, 0)
    dispatch(1, 0)

    def quarters(quarter, carry):
        @pl.when(quarter > 1)
        def _():
            prepare(0, quarter)

        dispatch(0, quarter, jnp.where(quarter == 1, 2, 0))
        prepare(1, quarter)
        dispatch(1, quarter)
        return carry

    for i in range(4, PLANES):
        fourier_load(i).wait()
    lax.fori_loop(1, PLANES // 2, quarters, 0)

    for load in loads:
        load.wait()
    sums[...] = jnp.zeros_like(sums)
    order[...] = gather_order()
    block, sample = places((NB, NR))
    spread[...] = ones_where(block == sample >> 3)
    sample, block = places((NR, NB))
    gather[...] = ones_where(block == sample >> 3)
    left, right = places((NB, NB))
    same = ones_where(left == right)

    def turned(value, by):
        return lax.dot_general(value, by, (((0,), (0,)), ((), ())), preferred_element_type=jnp.float32)

    for view in range(VIEWS):
        level = layer_in[view]
        layer[view] = turned(level.astype(jnp.float32).astype(jnp.bfloat16), same)
        added = jnp.zeros(level.shape, jnp.float32)
        for l in range(LAYERS):
            added = jnp.where(level == l, table_ref[view, l], added)
        cosine, sine = cos_sin(added)
        seen = level < LAYERS
        cosines[view] = sum(turned(part, spread[...]) for part in halves(jnp.where(seen, cosine, 0.0)))
        sines[view] = sum(turned(part, spread[...]) for part in halves(jnp.where(seen, sine, 0.0)))

    def angles(group, carry):
        here = pl.ds(pl.multiple_of(group * 16, 16), 16)
        own_cosine, own_sine = cos_sin(phase[:, here, :].astype(jnp.float32))
        wide_cosine, wide_sine = cosines[:, here, :], sines[:, here, :]
        cosines[:, here, :] = own_cosine * wide_cosine - own_sine * wide_sine
        sines[:, here, :] = own_sine * wide_cosine + own_cosine * wide_sine
        return carry

    lax.fori_loop(0, GROUPS, angles, 0)

    @pl.when(relays)
    def _():
        for half in LENT:
            pltpu.make_async_copy(lent.at[half], lent.at[half], lent_sem.at[half]).wait()

            def forward(n, carry):
                pass_on(half, n).start()
                return carry

            lax.fori_loop(0, PLANE, forward, 0)

    def gradients(n, carry):
        origin = entry_of(arrivals, n)
        hogels = PLANE * HOGELS
        here = pl.ds(pl.multiple_of(origin * hogels, hogels), hogels)
        for half in range(2):
            landed = recv.at[half, pl.ds(origin * PLANE, PLANE)]
            pltpu.make_async_copy(landed, landed, recv_sem.at[half, origin]).wait()
        came = [
            recv[:, pl.ds(origin * PLANE + first, GROUP), :, :].reshape(2 * GROUP * 16, NR) for first in (0, GROUP)
        ]
        ordered = dot(order[...], jnp.concatenate(came, 1))

        def part(rows):
            return jnp.concatenate([ordered[rows, i * NR : (i + 1) * NR].reshape(VIEWS, 16, NR) for i in range(2)], 1)

        real, imag = part(slice(0, 64)), part(slice(64, 128))
        cosine = cosines[:, here, :]
        sine = sines[:, here, :]
        term = amp[:, here, :].astype(jnp.float32) * (imag * cosine - real * sine)
        flat = term.reshape(VIEWS * hogels, NR)
        blocks = sum(dot(part, gather[...]) for part in halves(flat)).reshape(VIEWS, hogels, NB)
        grad_amp[:, here, :] = (real * cosine + imag * sine).astype(jnp.bfloat16)
        grad_phase[:, here, :] = term.astype(jnp.bfloat16)
        level = layer[:, here, :]
        for l in range(LAYERS):
            chosen = jnp.where(level == float(l), blocks, 0.0)
            sums[l] += jnp.sum(chosen.reshape(VIEWS, hogels // 8, 8, NB), axis=1)
        return carry

    lax.fori_loop(0, PLANES, gradients, 0)

    view_of, level_of = places((8, 128))
    own = jnp.zeros((8, 128), jnp.float32)
    for l in range(LAYERS):
        lane = jnp.sum(jnp.sum(sums[l], axis=1), axis=1, keepdims=True)
        lane = jnp.concatenate([lane, jnp.zeros((8 - VIEWS, 1), jnp.float32)], 0)
        own = jnp.where(level_of == l, lane, own)
    partial[0] = own

    @pl.when(upper == 0)
    def _():
        pl.semaphore_wait(rows_sem, ALONG)

    for n in range(1, ROWS):
        pltpu.make_async_remote_copy(
            src_ref=partial.at[0], dst_ref=partial.at[n], send_sem=row_send.at[n], recv_sem=row_recv.at[n],
            device_id={"rows": lax.rem(row + n, ROWS)}, device_id_type=MESH,
        ).start()

    for half in range(2):
        gone = stage.at[half, pl.ds(0, WIDE - 1)]
        pltpu.make_async_copy(gone, gone, send_sem.at[half]).wait()

    @pl.when(relays)
    def _():
        for half in LENT:
            pltpu.make_async_copy(lent.at[half], lent.at[half], passed_sem.at[half]).wait()

    @pl.when(me > 0)
    def _():
        halo.wait_send()

    total = own
    for n in range(1, ROWS):
        pltpu.make_async_copy(partial.at[n], partial.at[n], row_recv.at[n]).wait()
    for n in range(1, ROWS):
        total = total + partial[n]
        pltpu.make_async_copy(partial.at[0], partial.at[0], row_send.at[n]).wait()
    grad_layers_ref[...] = (total * (1.0 / math.sqrt(NR * ROWS * NH)))[:VIEWS, :LAYERS]


def hand_over(amp_in, phase_in, layers_in, amp_out, phase_out, layers_out, sem):
    copies = [pltpu.make_async_copy(layers_in, layers_out, sem.at[2 * VIEWS])]
    for view in range(VIEWS):
        copies.append(pltpu.make_async_copy(amp_in.at[view], amp_out.at[view], sem.at[view]))
        copies.append(pltpu.make_async_copy(phase_in.at[view], phase_out.at[view], sem.at[VIEWS + view]))
    for copy in copies:
        copy.start()
    for copy in copies:
        copy.wait()


def shards(cotangent, amplitude, view_phase, layer_block, layer_phase):
    anywhere = pl.BlockSpec(memory_space=pl.ANY)
    bf16, f32 = jnp.bfloat16, jnp.float32
    dma = pltpu.SemaphoreType.DMA
    grad_amp, grad_phase, grad_layers = grads = pl.pallas_call(
        kernel,
        out_shape=(
            pltpu.VMEM((VIEWS, NH, NR), bf16),
            pltpu.VMEM((VIEWS, NH, NR), bf16),
            pltpu.VMEM((VIEWS, LAYERS), f32),
        ),
        in_specs=[anywhere] * 6,
        out_specs=(pl.BlockSpec(memory_space=pltpu.VMEM),) * 3,
        scratch_shapes=[
            pltpu.VMEM((2, HOGELS * HALF, NR), f32),
            pltpu.VMEM((VIEWS, NH, NR), bf16),
            pltpu.VMEM((VIEWS, NH, NR), bf16),
            pltpu.VMEM((VIEWS, NB, NH), jnp.int32),
            pltpu.SMEM((VIEWS, LAYERS), f32),
            pltpu.VMEM((2 * HOG, 2 * HOG), f32),
            pltpu.VMEM((VIEWS, NH, NB), f32),
            pltpu.VMEM((NB, NR), bf16),
            pltpu.VMEM((NR, NB), bf16),
            pltpu.VMEM((128, 128), bf16),
            pltpu.VMEM((2, (HOGELS + 1) * HALF, NR), bf16),
            pltpu.VMEM((2, HOGELS * HALF, NR), bf16),
            pltpu.VMEM((2, WIDE, 16, NR), bf16),
            pltpu.VMEM((2, WIDE, 16, NR), bf16),
            pltpu.VMEM((2, PLANE, 16, NR), bf16),
            pltpu.VMEM((VIEWS, NH, NR), f32),
            pltpu.VMEM((VIEWS, NH, NR), f32),
            pltpu.VMEM((LAYERS, VIEWS, 8, NB), f32),
            pltpu.VMEM((ROWS, 8, 128), f32),
            dma((8,)), dma((PLANES,)), dma((2,)), dma((2, PLANES)), dma, dma, dma((ROWS,)), dma((ROWS,)),
            dma((2,)), dma((2,)), pltpu.SemaphoreType.REGULAR, pltpu.SemaphoreType.REGULAR,
        ],
        compiler_params=pltpu.CompilerParams(
            collective_id=0, has_side_effects=True, vmem_limit_bytes=61 * 1024 * 1024
        ),
    )(cotangent, amplitude, view_phase, jnp.swapaxes(layer_block, 1, 2), layer_phase.T, fourier_table())
    grad_amp, grad_phase, grad_layers = pl.pallas_call(
        hand_over,
        out_shape=tuple(jax.ShapeDtypeStruct(g.shape, g.dtype) for g in grads),
        in_specs=[pl.BlockSpec(memory_space=pltpu.VMEM)] * 3,
        out_specs=(anywhere,) * 3,
        scratch_shapes=[dma((2 * VIEWS + 1,))],
    )(*(pltpu.with_memory_space_constraint(g, pltpu.VMEM) for g in grads))
    return grad_amp, grad_phase, grad_layers.T


def solution(mesh):
    in_specs = (
        P(None, "wide", "rows"),
        P("wide", None, "rows"),
        P("wide", None, "rows"),
        P("wide", None, "rows"),
        P(None, "wide"),
    )
    out_specs = (P("wide", None, "rows"), P("wide", None, "rows"), P(None, "wide"))
    return jax.shard_map(shards, mesh=mesh, in_specs=in_specs, out_specs=out_specs, check_vma=False)
```

```python
import functools
import math

import jax
import jax.numpy as jnp
import numpy as np
from jax import lax
from jax.experimental import pallas as pl
from jax.experimental.pallas import tpu as pltpu
from jax.sharding import PartitionSpec as P

MESH = pl.DeviceIdType.MESH
HOG = 256
HALF = HOG // 2
LAYERS = 8
BLOCK = 8
WIDE = 64
ROWS = 8
VIEWS = 4
HOGELS = 4
NR = 384
NB = NR // BLOCK
NH = 256
GROUP = 4
GROUPS = WIDE // GROUP
PLANE = 8
PLANES = WIDE // PLANE
ALONG = 4
VISITS = (
    (4, 5, 6, 7, 1, 2, 3, 0),
    (4, 6, 7, 0, 5, 2, 3, 1),
    (0, 1, 3, 4, 2, 7, 6, 5),
    (0, 1, 2, 3, 4, 5, 6, 7),
    (0, 7, 1, 6, 2, 5, 3, 4),
    (0, 7, 2, 6, 1, 4, 3, 5),
    (1, 7, 0, 5, 3, 4, 2, 6),
    (0, 6, 1, 5, 3, 4, 2, 7),
    (4, 5, 6, 7, 1, 2, 3, 0),
    (4, 6, 7, 0, 5, 2, 3, 1),
    (0, 1, 3, 4, 2, 7, 6, 5),
    (0, 1, 2, 3, 4, 5, 6, 7),
    (0, 7, 1, 6, 2, 5, 3, 4),
    (0, 7, 2, 6, 1, 4, 3, 5),
    (1, 7, 0, 5, 3, 4, 2, 6),
    (3, 0, 1, 6, 5, 4, 2, 7),
)
LAST, UP, DOWN = PLANES - 1, 4, 3
LENT = (1,)
ARRIVALS = tuple(
    tuple(sorted(range(PLANES), key=lambda s: VISITS[half + s].index(d) // 2)) for half in (0, PLANES) for d in range(PLANES)
)
COS = (0.999999989, -0.499999891, 0.0416664892, -0.00138878035, 2.47698825e-05, -2.70790202e-07, 1.72450525e-09)
SIN = (0.999999999, -0.166666659, 0.00833332129, -0.000198405341, 2.75358492e-06, -2.47288044e-08, 1.36130722e-10)


def fourier_table():
    index = np.arange(HOG)
    angles = 2.0 * math.pi / HOG * (index[:, None] * index[None, :] % HOG)
    window = np.sin(math.pi * (index + 0.5) / HOG) ** 2 / math.sqrt(HOG)
    cosine = np.cos(angles) * window[None, :]
    sine = np.sin(angles) * window[None, :]
    table = np.stack([np.stack([cosine, sine], 1), np.stack([-sine, cosine], 1)], 0)
    table = table.reshape(2, WIDE, VIEWS, 2 * HOG).swapaxes(0, 1).reshape(2 * HOG, 2 * HOG)
    return table.astype(np.float32)


def places(shape):
    return (lax.broadcasted_iota(jnp.int32, shape, axis) for axis in range(2))


def ones_where(chosen):
    return jnp.where(chosen, 1.0, 0.0).astype(jnp.bfloat16)


def gather_order():
    goes, came = places((128, 128))
    part, view, source, half, hogel = goes >> 6, (goes >> 4) & 3, (goes >> 2) & 3, (goes >> 1) & 1, goes & 1
    return ones_where(came == half * 64 + source * 16 + hogel * 8 + part * 4 + view)


def polynomial(coefficients, square):
    total = jnp.full_like(square, coefficients[-1])
    for coefficient in coefficients[-2::-1]:
        total = total * square + coefficient
    return total


def cos_sin(angle):
    square = angle * angle
    return polynomial(COS, square), angle * polynomial(SIN, square)


def halves(value):
    high = value.astype(jnp.bfloat16)
    return high, (value - high.astype(jnp.float32)).astype(jnp.bfloat16)


def dot(a, b):
    return jnp.dot(a, b, preferred_element_type=jnp.float32)


def packed(orders, which):
    code = jnp.int32(0)
    for index, order in enumerate(orders):
        code = jnp.where(which == index, sum(entry << (3 * i) for i, entry in enumerate(order)), code)
    return code


def entry_of(code, i):
    return (code >> (3 * i)) & 7


def kernel(
    cot_hbm, amp_hbm, phase_hbm, layer_hbm, table_hbm, fourier_hbm,
    grad_amp, grad_phase, grad_layers_ref,
    cot, amp, phase, layer_in, table_ref, fourier, layer, spread, gather, order,
    xhigh, xlow, stage, recv, lent, cosines, sines, sums, partial,
    load_sem, fourier_sem, send_sem, recv_sem, halo_send, halo_recv, row_send, row_recv,
    lent_sem, passed_sem, wide_sem, rows_sem,
):
    me = lax.axis_index("wide")
    row = lax.axis_index("rows")
    plane, spot = me // PLANE, lax.rem(me, PLANE)
    upper, along = row // ALONG, lax.rem(row, ALONG)

    def greet(semaphore, **target):
        pl.semaphore_signal(semaphore, inc=1, device_id=target, device_id_type=MESH)

    def beside(n):
        return plane * PLANE + lax.rem(spot + n, PLANE)

    barrier = pltpu.get_barrier_semaphore()
    for n in range(1, PLANES):
        greet(barrier, wide=lax.rem(plane + n, PLANES) * PLANE + spot)
    for n in range(1, PLANE):
        greet(barrier, wide=beside(n))
    for n in range(1, ALONG):
        greet(barrier, rows=upper * ALONG + lax.rem(along + n, ALONG))

    @pl.when(upper == 0)
    def _():
        for n in range(ALONG):
            greet(barrier, rows=ALONG + n)

    relays = (upper == 0) & (plane == UP)
    relayed = (upper == 1) & (plane == LAST)
    rising = (plane == LAST) | (plane == UP)
    lender, borrower = jnp.where(rising, LAST, 0), jnp.where(rising, DOWN, UP)
    through = jnp.where(rising, UP, DOWN)

    @pl.when(relays)
    def _():
        greet(barrier, wide=lender * PLANE + spot, rows=ALONG + along)

    visits = packed(VISITS, upper * PLANES + plane)
    arrivals = packed(ARRIVALS, upper * PLANES + plane)

    early = pl.ds(0, (HOGELS - 1) * HALF)
    late = pl.ds((HOGELS - 1) * HALF, HALF)
    cot_loads = [
        pltpu.make_async_copy(cot_hbm.at[q, part], cot.at[q, part], load_sem.at[2 * i + q])
        for i, part in enumerate((early, late))
        for q in range(2)
    ]
    loads = [
        pltpu.make_async_copy(source, target, load_sem.at[4 + i])
        for i, (source, target) in enumerate((
            ((amp_hbm, amp), (phase_hbm, phase), (layer_hbm, layer_in), (table_hbm, table_ref))
        ))
    ]

    def rows_of(there):
        return pl.ds(pl.multiple_of(there * 64, 64), 64)

    def fourier_load(i):
        rows = rows_of(entry_of(visits, i))
        return pltpu.make_async_copy(fourier_hbm.at[rows], fourier.at[rows], fourier_sem.at[i])

    for load in cot_loads[:2]:
        load.start()
    for i in range(2):
        fourier_load(i).start()
    for load in cot_loads[2:]:
        load.start()
    for i in range(2, PLANES):
        fourier_load(i).start()
    for load in loads:
        load.start()

    def ready(part, copies):
        for copy in copies:
            copy.wait()
        high, low = halves(cot[:, part, :])
        xhigh[:, part, :] = high
        xlow[:, part, :] = low

    def transform(there, hogel):
        thigh, tlow = halves(fourier[rows_of(there), :])
        first, last = hogel * HALF, hogel * HALF + HOG
        total = None
        for q in range(2):
            columns = slice(q * HOG, q * HOG + HOG)
            terms = [dot(thigh[:, columns], xhigh[q, first:last, :]), dot(tlow[:, columns], xhigh[q, first:last, :])]
            known = min(last, HOGELS * HALF)
            terms.append(dot(thigh[:, q * HOG : q * HOG + known - first], xlow[q, first:known, :]))
            for term in terms:
                total = term if total is None else total + term
        return total.reshape(PLANE, 8, NR)

    def send(half, other):
        return pltpu.make_async_remote_copy(
            src_ref=stage.at[half, other], dst_ref=recv.at[half, me], send_sem=send_sem.at[half],
            recv_sem=recv_sem.at[half, plane], device_id={"wide": other}, device_id_type=MESH,
        )

    def keep(half):
        return pltpu.make_async_copy(stage.at[half, me], recv.at[half, me], recv_sem.at[half, plane])

    def prepare(half, quarter):
        for side in range(2):
            there = entry_of(visits, 2 * quarter + side)
            both = [transform(there, 2 * half + hogel) for hogel in range(2)]
            chunk = pl.ds(pl.multiple_of(there * PLANE, PLANE), PLANE)
            stage[half, chunk] = jnp.concatenate(both, 1).astype(jnp.bfloat16)

    def lend(half):
        return pltpu.make_async_remote_copy(
            src_ref=stage.at[half, pl.ds(borrower * PLANE, PLANE)], dst_ref=lent.at[half], send_sem=send_sem.at[half],
            recv_sem=lent_sem.at[half], device_id={"wide": through * PLANE + spot, "rows": along}, device_id_type=MESH,
        )

    def pass_on(half, n):
        return pltpu.make_async_remote_copy(
            src_ref=lent.at[half, n], dst_ref=recv.at[half, lender * PLANE + spot], send_sem=passed_sem.at[half],
            recv_sem=recv_sem.at[half, lender], device_id={"wide": borrower * PLANE + n, "rows": ALONG + along}, device_id_type=MESH,
        )

    def dispatch(half, quarter, first=0, last=2 * PLANE):
        @pl.when(relayed & (quarter == 0) & (half in LENT) & (last > 2))
        def _():
            lend(half).start()

        def step(n, carry):
            there = entry_of(visits, 2 * quarter + lax.rem(n, 2))
            other = there * PLANE + lax.rem(spot + n // 2, PLANE)

            @pl.when((other != me) & ~(relayed & (there == borrower) & (half in LENT)))
            def _():
                send(half, other).start()

            @pl.when(other == me)
            def _():
                keep(half).start()

            return carry

        lax.fori_loop(first, last, step, 0)

    halo = pltpu.make_async_remote_copy(
        src_ref=xhigh.at[:, pl.ds(0, HALF)], dst_ref=xhigh.at[:, pl.ds(HOGELS * HALF, HALF)],
        send_sem=halo_send, recv_sem=halo_recv,
        device_id={"wide": lax.rem(me + WIDE - 1, WIDE)}, device_id_type=MESH,
    )

    ready(early, cot_loads[:2])
    for i in range(2):
        fourier_load(i).wait()
    prepare(0, 0)

    pl.semaphore_wait(barrier, PLANES + PLANE + ALONG - 3 + ALONG * upper + relayed.astype(jnp.int32))
    for n in range(1, PLANE):
        greet(wide_sem, wide=beside(n))

    dispatch(0, 0, 0, 2)
    for i in (2, 3):
        fourier_load(i).wait()
    prepare(0, 1)
    dispatch(0, 1, 0, 2)
    @pl.when(upper == 1)
    def _():
        for n in range(ALONG):
            greet(rows_sem, rows=n)

    pl.semaphore_wait(wide_sem, PLANE - 1)

    @pl.when(me > 0)
    def _():
        halo.start()

    dispatch(0, 0, 2)
    ready(late, cot_loads[2:])

    @pl.when(me < WIDE - 1)
    def _():
        halo.wait_recv()

    @pl.when(me == WIDE - 1)
    def _():
        xhigh[:, pl.ds(HOGELS * HALF, HALF), :] = jnp.zeros((2, HALF, NR), jnp.bfloat16)

    prepare(1, 0)
    dispatch(1, 0)

    def quarters(quarter, carry):
        @pl.when(quarter > 1)
        def _():
            prepare(0, quarter)

        dispatch(0, quarter, jnp.where(quarter == 1, 2, 0))
        prepare(1, quarter)
        dispatch(1, quarter)
        return carry

    for i in range(4, PLANES):
        fourier_load(i).wait()
    lax.fori_loop(1, PLANES // 2, quarters, 0)

    for load in loads:
        load.wait()
    sums[...] = jnp.zeros_like(sums)
    order[...] = gather_order()
    block, sample = places((NB, NR))
    spread[...] = ones_where(block == sample >> 3)
    sample, block = places((NR, NB))
    gather[...] = ones_where(block == sample >> 3)
    left, right = places((NB, NB))
    same = ones_where(left == right)

    def turned(value, by):
        return lax.dot_general(value, by, (((0,), (0,)), ((), ())), preferred_element_type=jnp.float32)

    for view in range(VIEWS):
        level = layer_in[view]
        layer[view] = turned(level.astype(jnp.float32).astype(jnp.bfloat16), same)
        added = jnp.zeros(level.shape, jnp.float32)
        for l in range(LAYERS):
            added = jnp.where(level == l, table_ref[view, l], added)
        cosine, sine = cos_sin(added)
        seen = level < LAYERS
        cosines[view] = sum(turned(part, spread[...]) for part in halves(jnp.where(seen, cosine, 0.0)))
        sines[view] = sum(turned(part, spread[...]) for part in halves(jnp.where(seen, sine, 0.0)))

    def angles(group, carry):
        here = pl.ds(pl.multiple_of(group * 16, 16), 16)
        own_cosine, own_sine = cos_sin(phase[:, here, :].astype(jnp.float32))
        wide_cosine, wide_sine = cosines[:, here, :], sines[:, here, :]
        cosines[:, here, :] = own_cosine * wide_cosine - own_sine * wide_sine
        sines[:, here, :] = own_sine * wide_cosine + own_cosine * wide_sine
        return carry

    lax.fori_loop(0, GROUPS, angles, 0)

    @pl.when(relays)
    def _():
        for half in LENT:
            pltpu.make_async_copy(lent.at[half], lent.at[half], lent_sem.at[half]).wait()

            def forward(n, carry):
                pass_on(half, n).start()
                return carry

            lax.fori_loop(0, PLANE, forward, 0)

    def gradients(n, carry):
        origin = entry_of(arrivals, n)
        hogels = PLANE * HOGELS
        here = pl.ds(pl.multiple_of(origin * hogels, hogels), hogels)
        for half in range(2):
            landed = recv.at[half, pl.ds(origin * PLANE, PLANE)]
            pltpu.make_async_copy(landed, landed, recv_sem.at[half, origin]).wait()
        came = [
            recv[:, pl.ds(origin * PLANE + first, GROUP), :, :].reshape(2 * GROUP * 16, NR) for first in (0, GROUP)
        ]
        ordered = dot(order[...], jnp.concatenate(came, 1))

        def part(rows):
            return jnp.concatenate([ordered[rows, i * NR : (i + 1) * NR].reshape(VIEWS, 16, NR) for i in range(2)], 1)

        real, imag = part(slice(0, 64)), part(slice(64, 128))
        cosine = cosines[:, here, :]
        sine = sines[:, here, :]
        term = amp[:, here, :].astype(jnp.float32) * (imag * cosine - real * sine)
        flat = term.reshape(VIEWS * hogels, NR)
        blocks = sum(dot(part, gather[...]) for part in halves(flat)).reshape(VIEWS, hogels, NB)
        grad_amp[:, here, :] = (real * cosine + imag * sine).astype(jnp.bfloat16)
        grad_phase[:, here, :] = term.astype(jnp.bfloat16)
        level = layer[:, here, :]
        for l in range(LAYERS):
            chosen = jnp.where(level == float(l), blocks, 0.0)
            sums[l] += jnp.sum(chosen.reshape(VIEWS, hogels // 8, 8, NB), axis=1)
        return carry

    lax.fori_loop(0, PLANES, gradients, 0)

    view_of, level_of = places((8, 128))
    own = jnp.zeros((8, 128), jnp.float32)
    for l in range(LAYERS):
        lane = jnp.sum(jnp.sum(sums[l], axis=1), axis=1, keepdims=True)
        lane = jnp.concatenate([lane, jnp.zeros((8 - VIEWS, 1), jnp.float32)], 0)
        own = jnp.where(level_of == l, lane, own)
    partial[0] = own

    @pl.when(upper == 0)
    def _():
        pl.semaphore_wait(rows_sem, ALONG)

    for n in (4, 3, 5, 2, 6, 1, 7):
        pltpu.make_async_remote_copy(
            src_ref=partial.at[0], dst_ref=partial.at[n], send_sem=row_send.at[n], recv_sem=row_recv.at[n],
            device_id={"rows": lax.rem(row + n, ROWS)}, device_id_type=MESH,
        ).start()

    for half in range(2):
        gone = stage.at[half, pl.ds(0, WIDE - 1)]
        pltpu.make_async_copy(gone, gone, send_sem.at[half]).wait()

    @pl.when(relays)
    def _():
        for half in LENT:
            pltpu.make_async_copy(lent.at[half], lent.at[half], passed_sem.at[half]).wait()

    @pl.when(me > 0)
    def _():
        halo.wait_send()

    total = own
    for n in range(1, ROWS):
        pltpu.make_async_copy(partial.at[n], partial.at[n], row_recv.at[n]).wait()
    for n in range(1, ROWS):
        total = total + partial[n]
        pltpu.make_async_copy(partial.at[0], partial.at[0], row_send.at[n]).wait()
    grad_layers_ref[...] = (total * (1.0 / math.sqrt(NR * ROWS * NH)))[:VIEWS, :LAYERS]


def hand_over(amp_in, phase_in, layers_in, amp_out, phase_out, layers_out, sem):
    copies = [pltpu.make_async_copy(layers_in, layers_out, sem.at[2 * VIEWS])]
    for view in range(VIEWS):
        copies.append(pltpu.make_async_copy(amp_in.at[view], amp_out.at[view], sem.at[view]))
        copies.append(pltpu.make_async_copy(phase_in.at[view], phase_out.at[view], sem.at[VIEWS + view]))
    for copy in copies:
        copy.start()
    for copy in copies:
        copy.wait()


def shards(cotangent, amplitude, view_phase, layer_block, layer_phase):
    anywhere = pl.BlockSpec(memory_space=pl.ANY)
    bf16, f32 = jnp.bfloat16, jnp.float32
    dma = pltpu.SemaphoreType.DMA
    grad_amp, grad_phase, grad_layers = grads = pl.pallas_call(
        kernel,
        out_shape=(
            pltpu.VMEM((VIEWS, NH, NR), bf16),
            pltpu.VMEM((VIEWS, NH, NR), bf16),
            pltpu.VMEM((VIEWS, LAYERS), f32),
        ),
        in_specs=[anywhere] * 6,
        out_specs=(pl.BlockSpec(memory_space=pltpu.VMEM),) * 3,
        scratch_shapes=[
            pltpu.VMEM((2, HOGELS * HALF, NR), f32),
            pltpu.VMEM((VIEWS, NH, NR), bf16),
            pltpu.VMEM((VIEWS, NH, NR), bf16),
            pltpu.VMEM((VIEWS, NB, NH), jnp.int32),
            pltpu.SMEM((VIEWS, LAYERS), f32),
            pltpu.VMEM((2 * HOG, 2 * HOG), f32),
            pltpu.VMEM((VIEWS, NH, NB), f32),
            pltpu.VMEM((NB, NR), bf16),
            pltpu.VMEM((NR, NB), bf16),
            pltpu.VMEM((128, 128), bf16),
            pltpu.VMEM((2, (HOGELS + 1) * HALF, NR), bf16),
            pltpu.VMEM((2, HOGELS * HALF, NR), bf16),
            pltpu.VMEM((2, WIDE, 16, NR), bf16),
            pltpu.VMEM((2, WIDE, 16, NR), bf16),
            pltpu.VMEM((2, PLANE, 16, NR), bf16),
            pltpu.VMEM((VIEWS, NH, NR), f32),
            pltpu.VMEM((VIEWS, NH, NR), f32),
            pltpu.VMEM((LAYERS, VIEWS, 8, NB), f32),
            pltpu.VMEM((ROWS, 8, 128), f32),
            dma((8,)), dma((PLANES,)), dma((2,)), dma((2, PLANES)), dma, dma, dma((ROWS,)), dma((ROWS,)),
            dma((2,)), dma((2,)), pltpu.SemaphoreType.REGULAR, pltpu.SemaphoreType.REGULAR,
        ],
        compiler_params=pltpu.CompilerParams(
            collective_id=0, has_side_effects=True, vmem_limit_bytes=61 * 1024 * 1024
        ),
    )(cotangent, amplitude, view_phase, jnp.swapaxes(layer_block, 1, 2), layer_phase.T, fourier_table())
    grad_amp, grad_phase, grad_layers = pl.pallas_call(
        hand_over,
        out_shape=tuple(jax.ShapeDtypeStruct(g.shape, g.dtype) for g in grads),
        in_specs=[pl.BlockSpec(memory_space=pltpu.VMEM)] * 3,
        out_specs=(anywhere,) * 3,
        scratch_shapes=[dma((2 * VIEWS + 1,))],
    )(*(pltpu.with_memory_space_constraint(g, pltpu.VMEM) for g in grads))
    return grad_amp, grad_phase, grad_layers.T


def solution(mesh):
    in_specs = (
        P(None, "wide", "rows"),
        P("wide", None, "rows"),
        P("wide", None, "rows"),
        P("wide", None, "rows"),
        P(None, "wide"),
    )
    out_specs = (P("wide", None, "rows"), P("wide", None, "rows"), P(None, "wide"))
    return jax.shard_map(shards, mesh=mesh, in_specs=in_specs, out_specs=out_specs, check_vma=False)
```
